512 devices in a mesh: shot: 128 (over x, z, y_hi, core), freq: 4 (over y_lo).
Axes of the slice: x: 4, y: 8 (y_hi: 2, y_lo: 4; y = y_hi * 4 + y_lo), z: 8, core: 2. Of those that a mesh axis runs over, the one named last changes fastest.
Arguments:
- traces: float32 [384, 256, 1024], P('shot', None, 'freq'), may hold values from -6 to 6
- live_mask: int32 [384, 256], P('shot'), may hold values 0 or 1
- offset_bin: int32 [384, 256, 1], P('shot'), may hold values from 0 to 511; in each aligned block of 768 rows (0 to 767, 768 to 1535, ..., all dimensions but the last counted through in order) at most 2 rows name the same one
- surface: float32 [2048, 256, 512], P('shot', None, 'freq'), may hold values from -2.5 to 2.5
- block_owner: int32 [2], replicated, may hold values from 0 to 127
- point_column: int32 [2, 16], replicated, may hold values from 0 to 255
- filters: float32 [512, 31], P('shot'), may hold values from -1 to 1
Outputs:
- primaries: float32 [512, 256, 1024], P('shot', None, 'freq')
The draws below stay inside these ranges and needn't reach their ends.
Inputs may be any that keep to these rules, and one draw needn't show every extreme that they name: `offset_bin`: among the traces of one group of 3 consecutive shots (the rows of one device) no bin holds more than 2 traces, and in every draw some group has a bin with exactly 2; every bin holds some trace.
All inputs are finite; a program needn't handle non-finite values. No bound on the sum of `live_mask` on one device may be relied on, other than what follows from the above.
Results may differ from the reference program's by a relative error of at most 0.0003.
Values sent between devices are 32-bit elements; how exact they have to be, the bound alone decides.
A program may use at most 64 MiB of HBM per device.

```python
import math
import jax
import jax.numpy as jnp
import numpy as np
from jax import lax

R = 256
NT = 1024
NF = 256
TAPS = 31
POINTS_BLK = 16
STEPS = 2
SHOT_DEV = 3
SHOTS = 384
POINTS = 2048
NBINS = 512
MOST = 2
GROUP_SLOTS = 256
N_SHOT = 128
N_FREQ = 4


def with_ends(drawn, own_key, low, high):
    longest = drawn.shape.index(max(drawn.shape))
    spots = []
    for shift in (0, 1):
        where = [jax.random.randint(jax.random.fold_in(own_key, axis), (), 0, length) for axis, length in enumerate(drawn.shape)]
        where[longest] = (where[longest] + shift) % drawn.shape[longest]
        spots.append(tuple(where))
    return drawn.at[spots[0]].set(low).at[spots[1]].set(high)


def shard_levels(own_key, extent, shards, low, top_value):
    factor_of = 1.0
    for position, parts in shards:
        steps = jax.random.uniform(jax.random.fold_in(jax.random.fold_in(own_key, 6), position), (parts,), jnp.float32, low / len(shards), top_value / len(shards))
        factor_of = factor_of * jnp.repeat(jnp.exp(steps), extent[position] // parts).reshape((-1,) + (1,) * (len(extent) - 1 - position))
    return factor_of


def deal_out(own_key, own, number, rows, count, top, reach, lean):
    order = jax.random.permutation(own_key, count)
    crowded, ordinary = shares(count, rows * top, reach, lean, True), shares(count, rows * top, reach, lean, False)
    places = jnp.arange(count)

    def named(lengths, offset_by):
        used = int((lengths > 0).sum())
        fixed = max(1, used // 4)
        shifted = fixed + (places - fixed + offset_by * (used - fixed)) % max(1, count - fixed)
        return jnp.zeros((count,), jnp.int32).at[order[jnp.where(places < fixed, places, shifted)]].set(jnp.asarray(lengths, jnp.int32))

    lengths = jnp.where(number % 4 == 0, named(crowded, number // 4), named(ordinary, number - number // 4 - 1))
    mixed = jax.random.permutation(jax.random.fold_in(own, 3), count)
    source_of, taker = mixed[0:count // 2 * 2:2], mixed[1:count // 2 * 2:2]
    margin = jnp.minimum(lengths[source_of] - 1, reach - lengths[taker]) // 2
    margin = jnp.where((source_of == order[0]) | (taker == order[0]) | (lengths[taker] == 0), 0, jnp.maximum(margin, 0))
    shifted = jax.random.randint(jax.random.fold_in(own, 4), (count // 2,), 0, 1 << 20) % (margin + 1)
    lengths = lengths.at[source_of].add(-shifted).at[taker].add(shifted)
    members = jnp.searchsorted(jnp.cumsum(lengths), jnp.arange(rows * top), side="right").astype(jnp.int32)
    grid = members.reshape(top, rows).T
    grid = grid[jax.random.permutation(jax.random.fold_in(own, 1), rows)]
    offset_by = jax.random.randint(jax.random.fold_in(own, 2), (rows, 1), 0, top)
    return jnp.take_along_axis(grid, (jnp.arange(top)[None, :] + offset_by) % top, axis=1)


def shares(number_of, total, bound, slope, full):
    portions = [(1 << 20) // math.isqrt(rank ** slope) + 1 for rank in range(1, number_of + 1)]
    largest = bound if full else min(bound, max(-(-total // number_of), total * portions[0] // sum(portions)))
    least = 1 if total - largest >= number_of - 1 else 0
    counts, spare = [largest] + [least] * (number_of - 1), total - largest - least * (number_of - 1)
    while spare > 0:
        free = [i for i in range(1, number_of) if counts[i] < largest] or [i for i in range(1, number_of) if counts[i] < bound]
        pool, remaining = sum([portions[i] for i in free]), spare
        for i in free:
            extra = min(bound - counts[i], max(1, remaining * portions[i] // pool), spare)
            counts[i] = counts[i] + extra
            spare = spare - extra
    return np.array(counts)


def noise(own_key, dims, scale, limit, cuts=(), kind=jnp.bfloat16):
    result = jax.random.normal(own_key, dims, jnp.float32) * scale
    if len(cuts) > 0:
        result = shard_levels(own_key, dims, cuts, -0.22, 0.18) * result
    return jnp.clip(result, min=-limit, max=limit).astype(kind)


def setup_inputs(seed: int = 0) -> dict:
    splits = jax.random.split(jax.random.key(seed), 8)
    traces = noise(splits[0], (SHOTS, R, NT), 1.0, 6.0, ((0, 128), (2, 4)), jnp.float32)
    live_mask = with_ends((jax.random.randint(splits[1], (SHOTS, R), 0, 8) < 7).astype(jnp.int32), jax.random.fold_in(splits[1], 1), 0, 1)
    offset_bin_keys = jax.random.split(jax.random.fold_in(splits[2], 1), SHOTS * R // (SHOT_DEV * R))
    offset_bin_turns = jax.random.permutation(jax.random.fold_in(splits[2], 3), SHOTS * R // (SHOT_DEV * R))
    offset_bin = jax.vmap(lambda own, number: deal_out(jax.random.fold_in(splits[2], 2), own, number, SHOT_DEV * R, NBINS, 1, MOST, 1))(offset_bin_keys, offset_bin_turns).reshape((SHOTS, R, 1))
    surface = noise(splits[3], (POINTS, R, 2 * NF), ((NT / (4 * STEPS * POINTS_BLK * NF)) ** 0.5), 2.5, ((0, 128), (2, 4)), jnp.float32)
    block_owner = jax.random.randint(splits[4], (STEPS,), 0, N_SHOT).astype(jnp.int32)
    point_column = with_ends(jax.random.randint(splits[5], (STEPS, POINTS_BLK), 0, R), jax.random.fold_in(splits[5], 1), 0, R - 1).astype(jnp.int32)
    filters = noise(splits[6], (NBINS, TAPS), TAPS ** -0.5, 1.0, ((0, 128),), jnp.float32)
    return dict(traces=traces, live_mask=live_mask, offset_bin=offset_bin, surface=surface, block_owner=block_owner, point_column=point_column, filters=filters)


FULL_PRECISION = lax.Precision.HIGHEST


def wave_table(time_ids, comp_ids, band_width, period):
    mode_ids = (comp_ids // (2 * band_width)) * band_width + comp_ids % band_width
    phase_ids = ((mode_ids[None, :] + 1) * time_ids[:, None]) % period
    angles = phase_ids.astype(jnp.float32) * (2.0 * math.pi / period)
    real_part = (comp_ids % (2 * band_width)) < band_width
    return jnp.where(real_part[None, :], jnp.cos(angles), -jnp.sin(angles))


def cross_mix(left_side, right_side):
    return jnp.einsum("sjgb,jrgb->srgb", left_side, right_side, precision=FULL_PRECISION)


def shifted_sum(widened, tap_table, out_width):
    half_span = (tap_table.shape[-1] - 1) // 2
    summed = jnp.zeros(widened.shape[:-1] + (out_width,), jnp.float32)
    for tap_index in range(tap_table.shape[-1]):
        offset_start = 2 * half_span - tap_index
        window = lax.slice_in_dim(widened, offset_start, offset_start + out_width, axis=widened.ndim - 1)
        summed = summed + tap_table[..., tap_index:tap_index + 1] * window
    return summed


def group_ranks(group_bins):
    order_ids = jnp.arange(group_bins.shape[0])
    earlier = (group_bins[:, None] == group_bins[None, :]) & (order_ids[None, :] < order_ids[:, None])
    return jnp.sum(earlier.astype(jnp.int32), axis=1)


def reference(traces, live_mask, offset_bin, surface, block_owner, point_column, filters):
    band_width = NF // N_FREQ
    live_rows = live_mask.astype(jnp.float32)[:, :, None]
    live_traces = traces * live_rows
    columns = point_column.reshape(-1)
    picked = live_traces[:, columns, :]
    table_full = wave_table(jnp.arange(NT), jnp.arange(2 * NF), band_width, NT)
    spectra = jnp.einsum("sjt,tc->sjc", picked, table_full, precision=FULL_PRECISION)
    spectra = spectra.reshape(SHOTS, STEPS * POINTS_BLK, N_FREQ, 2, band_width)
    real_sum = jnp.zeros((SHOTS, R, N_FREQ, band_width), jnp.float32)
    imag_sum = jnp.zeros((SHOTS, R, N_FREQ, band_width), jnp.float32)
    for step_index in range(STEPS):
        first_point = (block_owner[step_index] * POINTS_BLK).astype(jnp.int32)
        surface_part = lax.dynamic_slice_in_dim(surface, first_point, POINTS_BLK, 0)
        surface_part = surface_part.reshape(POINTS_BLK, R, N_FREQ, 2, band_width)
        point_spectra = spectra[:, step_index * POINTS_BLK:(step_index + 1) * POINTS_BLK]
        data_real = point_spectra[:, :, :, 0]
        data_imag = point_spectra[:, :, :, 1]
        surf_real = surface_part[:, :, :, 0]
        surf_imag = surface_part[:, :, :, 1]
        real_sum = real_sum + (cross_mix(data_real, surf_real) - cross_mix(data_imag, surf_imag))
        imag_sum = imag_sum + (cross_mix(data_real, surf_imag) + cross_mix(data_imag, surf_real))
    prediction = jnp.stack([real_sum, imag_sum], axis=3).reshape(SHOTS, R, 2 * NF)
    inverse = table_full.T * (2.0 / NT)
    multiples = jnp.einsum("src,ct->srt", prediction, inverse, precision=FULL_PRECISION) * live_rows
    half_span = (TAPS - 1) // 2
    widened = jnp.pad(multiples, ((0, 0), (0, 0), (half_span, half_span)))
    bins_full = offset_bin[:, :, 0]
    trace_taps = filters[bins_full]
    cleaned = live_traces - shifted_sum(widened, trace_taps, NT)
    rank_ids = lax.map(group_ranks, bins_full.reshape(N_SHOT, SHOT_DEV * R)).reshape(SHOTS, R)
    group_ids = (jnp.arange(SHOTS) // SHOT_DEV)[:, None]
    slot_ids = group_ids * MOST + rank_ids
    return jnp.zeros((NBINS, GROUP_SLOTS, NT), jnp.float32).at[bins_full, slot_ids].set(cleaned)
```

```python
import functools
import math

import jax
import jax.numpy as jnp
import numpy as np
from jax import lax
from jax.experimental import pallas as pl
from jax.experimental.pallas import tpu as pltpu
from jax.sharding import PartitionSpec as P

NT = 1024
NF = 256
TAPS = 31
POINTS_BLK = 16
STEPS = 2
NX, NZ, NH, NC = 4, 8, 2, 2
NQ = 4
BAND = NF // NQ
LANES = 2 * BAND
QUARTER = NT // NQ
R = 256
SHOTS = 3
ROWS = SHOTS * R
PIECES = NX * NC
CHUNKS = 4
SUB = 8
COLS = STEPS * POINTS_BLK
PAIR = POINTS_BLK // NZ
EDGE = (TAPS - 1) // 2
FULL = lax.Precision.HIGHEST
MESH = pl.DeviceIdType.MESH
F32 = jnp.float32


def tables():
    t = np.arange(NT)
    m = np.arange(NF) + 1
    phase = 2 * np.pi * ((m[:, None] * t[None, :]) % NT) / NT
    real = np.cos(phase).reshape(NQ, BAND, NT)
    imag = -np.sin(phase).reshape(NQ, BAND, NT)
    wave = np.concatenate([real, imag], axis=1).reshape(NQ * LANES, NT)
    forward = wave.T.reshape(NQ, QUARTER, NQ * LANES)
    synth = wave * (2.0 / NT)
    k = np.arange(64)
    u = np.arange(EDGE)
    turn = 2 * np.pi * ((u[:, None] * k[None, :]) % 64) / 64
    short = np.concatenate([np.cos(turn), -np.sin(turn)], axis=1)
    edge = np.zeros((NQ, NQ * LANES, 128))
    edge[0] = synth[:, NT - EDGE :] @ short
    edge[NQ - 1] = synth[:, :EDGE] @ short
    back = np.zeros((NQ, 128, QUARTER))

    def inverse(n):
        a = 2 * np.pi * ((k[:, None] * n[None, :]) % 64) / 64
        return -np.concatenate([np.cos(a), -np.sin(a)], axis=0) / 64

    back[0][:, :EDGE] = inverse(np.arange(2 * EDGE, 3 * EDGE))
    back[NQ - 1][:, QUARTER - EDGE :] = inverse(np.arange(EDGE))
    combine = np.concatenate(
        [synth.reshape(NQ * LANES, NQ, QUARTER).transpose(1, 0, 2), back], axis=1
    )
    i = np.arange(TAPS)
    lag = 2 * np.pi * (((i[:, None] - EDGE) * m[None, :]) % NT) / NT
    c, s = np.cos(lag).reshape(TAPS, NQ, BAND), np.sin(lag).reshape(TAPS, NQ, BAND)
    same = np.concatenate([c, c], axis=2).reshape(TAPS, NQ * LANES)
    cross = np.concatenate([s, -s], axis=2).reshape(TAPS, NQ * LANES)
    lag2 = 2 * np.pi * ((i[:, None] * k[None, :]) % 64) / 64
    same2 = np.concatenate([np.cos(lag2), np.cos(lag2)], axis=1)
    cross2 = np.concatenate([np.sin(lag2), -np.sin(lag2)], axis=1)
    taps = np.concatenate([same, same2, cross, cross2], axis=1)
    taps = np.concatenate([taps] * 4 + [np.zeros((4, taps.shape[1]))], axis=0)
    return [np.asarray(a, np.float32) for a in (forward, edge, combine, taps)]


FORWARD, EDGE_IN, COMBINE, TAP_TABLE = tables()


def place():
    d = lax.axis_index("shot")
    x, z = d // (NZ * NH * NC), d // (NH * NC) % NZ
    return x, z, d // NC % NH, d % NC, lax.axis_index("freq")


def shot_of(x, z, h, c):
    return ((x * NZ + z) * NH + h) * NC + c


def spread_kernel(
    traces, live, cols, wave, surface, weights, filt, bands, table,
    r1, m, r2, hown, hin, ag, specp, specr, specall, sa, sb, srot, pred, f1, f1c,
    s1s, s1r, s2s, s2r, hs, hr, gs, gr, bs, br, fs, fr,
    ps, pr, cs, cr, u1s, u1r, u2s, u2r, us, ur, own,
):
    x, z, h, c, f = place()
    mine = x * NC + c

    def dev_p(j):
        p = lax.rem(mine + j, PIECES)
        return p, (shot_of(p // NC, z, h, lax.rem(p, NC)), f)

    def dev_z(j):
        o = lax.rem(z + j, NZ)
        return o, (shot_of(x, o, h, c), f)

    def dev_f(j):
        o = lax.rem(f + j, NQ)
        return o, (shot_of(x, z, h, c), o)

    other_h = (shot_of(x, z, 1 - h, c), f)

    barrier = pltpu.get_barrier_semaphore()

    def greet(dev):
        pl.semaphore_signal(barrier, inc=1, device_id=dev, device_id_type=MESH)

    def each(count, fn):
        def body(j, _):
            fn(j)
            return 0

        lax.fori_loop(1, count, body, 0)

    each(PIECES, lambda j: greet(dev_p(j)[1]))
    each(NZ, lambda j: greet(dev_z(j)[1]))
    each(NQ, lambda j: greet(dev_f(j)[1]))
    greet(other_h)
    pl.semaphore_wait(barrier, PIECES - 1 + NZ - 1 + NQ - 1 + 1)

    def remote(src, dst, send, recv, dev):
        return pltpu.make_async_remote_copy(
            src_ref=src, dst_ref=dst, send_sem=send, recv_sem=recv,
            device_id=dev, device_id_type=MESH,
        )

    def first(k, j, at):
        p, dev = dev_p(j)
        src = surface.at[:, pl.ds(pl.multiple_of(p * (CHUNKS * SUB) + k * SUB, SUB), SUB), :]
        return remote(src, r1.at[k, at(p)], s1s.at[k, p], s1r.at[k, at(p)], dev)

    def second(k, j, at):
        o, dev = dev_z(j)
        return remote(
            m.at[k, :, pl.ds(o * PAIR, PAIR)], r2.at[k, at(o)], s2s.at[k, o], s2r.at[k, at(o)], dev
        )

    def third(k):
        return remote(hown.at[k], hin.at[k], hs.at[k], hr.at[k], other_h)

    def fourth(k, j, at):
        o, dev = dev_z(j)
        return remote(ag.at[k, z], ag.at[k, at(o)], gs.at[k, o], gr.at[k, at(o)], dev)

    def fifth(k, j, at):
        p, dev = dev_p(j)
        return remote(
            pred.at[p, :, k], bands.at[f, :, at(p), k], bs.at[k, p], br.at[k, at(p)], dev
        )

    def sixth(k, j, at):
        o, dev = dev_f(j)
        return remote(
            bands.at[f, :, :, k], bands.at[at(o), :, :, k], fs.at[k, o], fr.at[k, at(o)], dev
        )

    def spec_f(j, at):
        o, dev = dev_f(j)
        return remote(specp.at[o], specr.at[at(o)], ps.at[o], pr.at[at(o)], dev)

    def spec_p(j, at):
        p, dev = dev_p(j)
        return remote(specall.at[mine], specall.at[at(p)], cs.at[p], cr.at[at(p)], dev)

    def filt_p(j, at):
        p, dev = dev_p(j)
        return remote(filt, f1.at[at(p)], u1s.at[p], u1r.at[at(p)], dev)

    def filt_z(j, at):
        o, dev = dev_z(j)
        return remote(f1c, table.at[h, at(o)], u2s.at[o], u2r.at[at(o)], dev)

    def filt_h(at):
        return remote(table.at[h], table.at[at], us, ur, other_h)

    def to_p(p):
        return mine

    def to_z(o):
        return z

    def to_f(o):
        return f

    def here(o):
        return o

    each(PIECES, lambda j: filt_p(j, to_p).start())

    def start_first(k, _):
        each(PIECES, lambda j: first(k, j, to_p).start())
        return 0

    lax.fori_loop(0, CHUNKS, start_first, 0)

    def own_piece(k):
        src = surface.at[:, pl.ds(pl.multiple_of(mine * (CHUNKS * SUB) + k * SUB, SUB), SUB), :]
        return pltpu.make_async_copy(src, r1.at[k, mine], own.at[k])

    for k in range(CHUNKS):
        own_piece(k).start()

    at_point = lax.broadcasted_iota(jnp.int32, (COLS, R), 1) == cols[...]
    for s in range(SHOTS):
        pick = jnp.where(at_point, live[s : s + 1, :], 0.0)
        picked = jnp.dot(pick, traces[s], precision=FULL, preferred_element_type=F32)
        part = jnp.dot(picked, wave[...], precision=FULL, preferred_element_type=F32)
        for o in range(NQ):
            specp[o, s * COLS : (s + 1) * COLS, :] = part[:, o * LANES : (o + 1) * LANES]
    each(NQ, lambda j: spec_f(j, to_f).start())
    specr[f] = specp[f]

    f1[mine] = filt[...]
    each(PIECES, lambda j: filt_p(j, here).wait_recv())
    for p in range(PIECES):
        f1c[p : p + 1, :] = f1[p, 0:1, :]
    each(NZ, lambda j: filt_z(j, to_z).start())

    each(NQ, lambda j: spec_f(j, here).wait_recv())
    specall[mine] = specr[0] + specr[1] + specr[2] + specr[3]
    each(PIECES, lambda j: spec_p(j, to_p).start())

    table[h, z] = f1c[...]
    each(NZ, lambda j: filt_z(j, here).wait_recv())
    filt_h(h).start()

    each(PIECES, lambda j: spec_p(j, here).wait_recv())
    low = lax.broadcasted_iota(jnp.int32, (SHOTS * COLS, LANES), 1) < BAND

    def both(p, _):
        v = specall[p]
        w = pltpu.roll(v, BAND, 1)
        sa[p] = jnp.where(low, v, w)
        sb[p] = jnp.where(low, -w, v)
        return 0

    lax.fori_loop(0, PIECES, both, 0)

    def predict(k):
        each(NZ, lambda j: fourth(k, j, here).wait_recv())
        srot[...] = pltpu.roll(
            ag[k].reshape(NZ * STEPS * PAIR * SUB, LANES), BAND, 1
        ).reshape(NZ, STEPS, PAIR, SUB, LANES)

        def piece(p, _):
            totals = [jnp.zeros((SUB, LANES), F32) for _ in range(SHOTS)]
            for o in range(NZ):
                for b in range(STEPS):
                    for i in range(PAIR):
                        straight, turned = ag[k, o, b, i], srot[o, b, i]
                        for s in range(SHOTS):
                            row = s * COLS + b * POINTS_BLK + o * PAIR + i
                            totals[s] = (
                                totals[s]
                                + sa[p, row : row + 1, :] * straight
                                + sb[p, row : row + 1, :] * turned
                            )
            for s in range(SHOTS):
                pred[p, s, k] = totals[s]
            return 0

        lax.fori_loop(0, PIECES, piece, 0)
        each(PIECES, lambda j: fifth(k, j, to_p).start())
        for s in range(SHOTS):
            bands[f, s, mine, k] = pred[mine, s, k]

    def choose(k):
        own_piece(k).wait()
        each(PIECES, lambda j: first(k, j, here).wait_recv())
        for b in range(STEPS):
            total = jnp.zeros((POINTS_BLK, SUB, LANES), F32)
            for p in range(PIECES):
                total = total + weights[b, p] * r1[k, p]
            m[k, b] = total
        each(NZ, lambda j: second(k, j, to_z).start())
        for b in range(STEPS):
            r2[k, z, b] = m[k, b, pl.ds(z * PAIR, PAIR)]

    def gather(k):
        each(PIECES, lambda j: fifth(k, j, here).wait_recv())
        each(NQ, lambda j: sixth(k, j, to_f).start())

    def across(k):
        each(NZ, lambda j: second(k, j, here).wait_recv())
        for b in range(STEPS):
            total = jnp.zeros((PAIR, SUB, LANES), F32)
            for o in range(NZ):
                total = total + weights[b, PIECES + o] * r2[k, o, b]
            hown[k, b] = total
        third(k).start()

    def share(k):
        third(k).wait_recv()
        for b in range(STEPS):
            ag[k, z, b] = (
                weights[b, PIECES + NZ] * hown[k, b] + weights[b, PIECES + NZ + 1] * hin[k, b]
            )
        each(NZ, lambda j: fourth(k, j, to_z).start())

    def tick(t, _):
        @pl.when(t >= 1)
        def _():
            predict(t - 1)

        @pl.when(t < CHUNKS)
        def _():
            choose(t)

        @pl.when(t >= 1)
        def _():
            gather(t - 1)

        @pl.when(t < CHUNKS)
        def _():
            across(t)
            share(t)

        return 0

    lax.fori_loop(0, CHUNKS + 1, tick, 0)

    filt_h(1 - h).wait_recv()

    def finish(k, _):
        each(NQ, lambda j: sixth(k, j, here).wait_recv())
        each(PIECES, lambda j: first(k, j, to_p).wait_send())
        each(NZ, lambda j: second(k, j, to_z).wait_send())
        third(k).wait_send()
        each(NZ, lambda j: fourth(k, j, to_z).wait_send())
        each(PIECES, lambda j: fifth(k, j, to_p).wait_send())
        each(NQ, lambda j: sixth(k, j, to_f).wait_send())
        return 0

    lax.fori_loop(0, CHUNKS, finish, 0)
    each(NQ, lambda j: spec_f(j, to_f).wait_send())
    each(PIECES, lambda j: spec_p(j, to_p).wait_send())
    each(PIECES, lambda j: filt_p(j, to_p).wait_send())
    each(NZ, lambda j: filt_z(j, to_z).wait_send())
    filt_h(h).wait_send()


def spread(traces, live, cols, wave, surface, weights, filt):
    dma = pltpu.SemaphoreType.DMA
    v = pltpu.VMEM
    tile = (SUB, LANES)
    vm = pl.BlockSpec(memory_space=pltpu.VMEM)
    small = (STEPS, PAIR, *tile)
    return pl.pallas_call(
        spread_kernel,
        out_shape=(
            jax.ShapeDtypeStruct((NQ, SHOTS, PIECES, CHUNKS, *tile), F32),
            jax.ShapeDtypeStruct((NH, NZ, PIECES, 128), F32),
        ),
        in_specs=[
            vm, vm, vm, vm,
            pl.BlockSpec(memory_space=pl.ANY),
            pl.BlockSpec(memory_space=pltpu.SMEM),
            vm,
        ],
        out_specs=(vm, vm),
        scratch_shapes=[
            v((CHUNKS, PIECES, POINTS_BLK, *tile), F32),
            v((CHUNKS, STEPS, POINTS_BLK, *tile), F32),
            v((CHUNKS, NZ, *small), F32),
            v((CHUNKS, *small), F32),
            v((CHUNKS, *small), F32),
            v((CHUNKS, NZ, *small), F32),
            v((NQ, SHOTS * COLS, LANES), F32),
            v((NQ, SHOTS * COLS, LANES), F32),
            v((PIECES, SHOTS * COLS, LANES), F32),
            v((PIECES, SHOTS * COLS, LANES), F32),
            v((PIECES, SHOTS * COLS, LANES), F32),
            v((NZ, *small), F32),
            v((PIECES, SHOTS, CHUNKS, *tile), F32),
            v((PIECES, 8, 128), F32),
            v((PIECES, 128), F32),
            dma((CHUNKS, PIECES)), dma((CHUNKS, PIECES)),
            dma((CHUNKS, NZ)), dma((CHUNKS, NZ)),
            dma((CHUNKS,)), dma((CHUNKS,)),
            dma((CHUNKS, NZ)), dma((CHUNKS, NZ)),
            dma((CHUNKS, PIECES)), dma((CHUNKS, PIECES)),
            dma((CHUNKS, NQ)), dma((CHUNKS, NQ)),
            dma((NQ,)), dma((NQ,)),
            dma((PIECES,)), dma((PIECES,)),
            dma((PIECES,)), dma((PIECES,)),
            dma((NZ,)), dma((NZ,)),
            dma, dma,
            dma((CHUNKS,)),
        ],
        compiler_params=pltpu.CompilerParams(
            collective_id=0, has_side_effects=True, vmem_limit_bytes=40 * 2**20
        ),
    )(traces, live, cols, wave, surface, weights, filt)


TILE = 192


def clean_kernel(
    bands, table, rowids, live, traces, slots, edge, combine, taps, out, cleaned
):
    def rows(i, _):
        at = pl.ds(pl.multiple_of(i * TILE, TILE), TILE)
        lane = lax.broadcasted_iota(jnp.int32, (TILE, 128), 1)
        ids = rowids[at, :]
        pick = jnp.where(lane == ids[:, 0:1], 1.0, 0.0)
        four = jnp.dot(pick, table[...], precision=FULL, preferred_element_type=F32)
        low = ids[:, 1:2]
        four = jnp.where((lane >= low) & (lane < low + TAPS), four, 0.0)
        factor = jnp.dot(four, taps[...], precision=FULL, preferred_element_type=F32)
        blocks = [bands[o, at, :] for o in range(NQ)]
        ends = jnp.zeros((TILE, 128), F32)
        for o in range(NQ):
            ends = ends + jnp.dot(
                blocks[o], edge[o * LANES : (o + 1) * LANES, :],
                precision=FULL, preferred_element_type=F32,
            )
        blocks.append(ends)
        total = jnp.zeros((TILE, QUARTER), F32)
        width = (NQ + 1) * LANES
        for o in range(NQ + 1):
            span = slice(o * LANES, (o + 1) * LANES)
            cross = slice(width + o * LANES, width + (o + 1) * LANES)
            mixed = blocks[o] * factor[:, span]
            mixed = mixed + pltpu.roll(blocks[o], BAND, 1) * factor[:, cross]
            total = total + jnp.dot(
                mixed, combine[span, :], precision=FULL, preferred_element_type=F32
            )
        cleaned[at, :] = live[at, :] * (traces[at, :] - total)
        return 0

    lax.fori_loop(0, ROWS // TILE, rows, 0)

    def place_rows(i, _):
        ids = lax.broadcasted_iota(jnp.int32, (128, ROWS), 0) + i * 128
        pick = jnp.where(ids == slots[...], 1.0, 0.0)
        out[pl.ds(pl.multiple_of(i * 128, 128), 128), :] = jnp.dot(
            pick, cleaned[...], precision=FULL, preferred_element_type=F32
        )
        return 0

    lax.fori_loop(0, out.shape[0] // 128, place_rows, 0)


def clean(*args):
    vm = pl.BlockSpec(memory_space=pltpu.VMEM)
    return pl.pallas_call(
        clean_kernel,
        out_shape=jax.ShapeDtypeStruct((1024, QUARTER), F32),
        in_specs=[vm] * len(args),
        out_specs=vm,
        scratch_shapes=[pltpu.VMEM((ROWS, QUARTER), F32)],
        compiler_params=pltpu.CompilerParams(vmem_limit_bytes=40 * 2**20),
    )(*args)


def on_device(traces, live_mask, offset_bin, surface, block_owner, point_column, filters):
    x, z, h, c, f = place()
    live = live_mask.astype(F32)
    owner = block_owner[:, None]
    piece = owner // (NZ * NH * NC) * NC + owner % NC
    same_h = owner // NC % NH == h
    weights = jnp.concatenate(
        [
            piece == jnp.arange(PIECES)[None, :],
            owner // (NH * NC) % NZ == jnp.arange(NZ)[None, :],
            same_h,
            ~same_h,
        ],
        axis=1,
    ).astype(F32)
    filt = jnp.pad(filters.reshape(1, 4 * TAPS), ((0, 7), (0, 128 - 4 * TAPS)))
    wave = lax.dynamic_index_in_dim(jnp.asarray(FORWARD), f, 0, keepdims=False)
    edge = lax.dynamic_index_in_dim(jnp.asarray(EDGE_IN), f, 0, keepdims=False)
    combine = lax.dynamic_index_in_dim(jnp.asarray(COMBINE), f, 0, keepdims=False)
    bands, table = spread(
        traces, live, point_column.reshape(COLS, 1), wave, surface, weights, filt
    )
    bins = offset_bin.reshape(ROWS)
    order = jnp.arange(ROWS)
    earlier = (bins[:, None] == bins[None, :]) & (order[None, :] < order[:, None])
    slots = bins * 2 + jnp.sum(earlier.astype(jnp.int32), axis=1)
    home = bins // 4
    row = home // NC % NH * (NZ * PIECES) + home // (NH * NC) % NZ * PIECES
    row = row + home // (NZ * NH * NC) * NC + home % NC
    rowids = jnp.stack([row, bins % 4 * TAPS], axis=1)
    packed = clean(
        bands.reshape(NQ, ROWS, LANES),
        table.reshape(128, 128),
        rowids,
        live.reshape(ROWS, 1),
        traces.reshape(ROWS, QUARTER),
        slots.reshape(1, ROWS),
        edge,
        combine,
        jnp.asarray(TAP_TABLE),
    )
    packed = packed.reshape(128, 8, QUARTER)
    dealt = lax.all_to_all(packed, "shot", split_axis=0, concat_axis=0, tiled=True)
    dealt = dealt.reshape(128, 4, 2, QUARTER).transpose(1, 0, 2, 3)
    return dealt.reshape(4, 256, QUARTER)


def solution(mesh):
    return jax.shard_map(
        on_device,
        mesh=mesh,
        in_specs=(
            P("shot", None, "freq"),
            P("shot", None),
            P("shot", None, None),
            P("shot", None, "freq"),
            P(),
            P(),
            P("shot", None),
        ),
        out_specs=P("shot", None, "freq"),
        check_vma=False,
    )
```

```python
import jax
import jax.numpy as jnp
import ml_dtypes
import numpy as np
from jax import lax
from jax.experimental import pallas as pl
from jax.experimental.pallas import tpu as pltpu
from jax.sharding import PartitionSpec as P

NT = 1024
NF = 256
TAPS = 31
POINTS_BLK = 16
STEPS = 2
NX, NZ, NH, NC = 4, 8, 2, 2
NQ = 4
BAND = NF // NQ
LANES = 2 * BAND
QUARTER = NT // NQ
R = 256
SHOTS = 3
ROWS = SHOTS * R
PIECES = NX * NC
CHUNKS = 4
SUB = 8
COLS = STEPS * POINTS_BLK
PAIR = POINTS_BLK // NZ
EDGE = (TAPS - 1) // 2
FULL = lax.Precision.HIGHEST
MESH = pl.DeviceIdType.MESH
F32 = jnp.float32
B16 = jnp.bfloat16
I32 = jnp.int32


def tables():
    t = np.arange(NT)
    m = np.arange(NF) + 1
    phase = 2 * np.pi * ((m[:, None] * t[None, :]) % NT) / NT
    real = np.cos(phase).reshape(NQ, BAND, NT)
    imag = -np.sin(phase).reshape(NQ, BAND, NT)
    wave = np.concatenate([real, imag], axis=1).reshape(NQ * LANES, NT)
    forward = wave.T.reshape(NQ, QUARTER, NQ * LANES)
    synth = wave * (2.0 / NT)
    k = np.arange(64)
    u = np.arange(EDGE)
    turn = 2 * np.pi * ((u[:, None] * k[None, :]) % 64) / 64
    short = np.concatenate([np.cos(turn), -np.sin(turn)], axis=1)
    edge = np.zeros((NQ, NQ * LANES, 128))
    edge[0] = synth[:, NT - EDGE :] @ short
    edge[NQ - 1] = synth[:, :EDGE] @ short
    back = np.zeros((NQ, 128, QUARTER))

    def inverse(n):
        a = 2 * np.pi * ((k[:, None] * n[None, :]) % 64) / 64
        return -np.concatenate([np.cos(a), -np.sin(a)], axis=0) / 64

    back[0][:, :EDGE] = inverse(np.arange(2 * EDGE, 3 * EDGE))
    back[NQ - 1][:, QUARTER - EDGE :] = inverse(np.arange(EDGE))
    combine = np.concatenate(
        [synth.reshape(NQ * LANES, NQ, QUARTER).transpose(1, 0, 2), back], axis=1
    )
    i = np.arange(TAPS)
    lag = 2 * np.pi * (((i[:, None] - EDGE) * m[None, :]) % NT) / NT
    c, s = np.cos(lag).reshape(TAPS, NQ, BAND), np.sin(lag).reshape(TAPS, NQ, BAND)
    same = np.concatenate([c, c], axis=2).reshape(TAPS, NQ * LANES)
    cross = np.concatenate([s, -s], axis=2).reshape(TAPS, NQ * LANES)
    lag2 = 2 * np.pi * ((i[:, None] * k[None, :]) % 64) / 64
    same2 = np.concatenate([np.cos(lag2), np.cos(lag2)], axis=1)
    cross2 = np.concatenate([np.sin(lag2), -np.sin(lag2)], axis=1)
    taps = np.concatenate([same, same2, cross, cross2], axis=1)
    taps = np.concatenate([taps] * 4 + [np.zeros((4, taps.shape[1]))], axis=0)
    return forward, edge, combine, taps


def halves(a):
    top = a.astype(ml_dtypes.bfloat16)
    return top, (a - top.astype(np.float64)).astype(ml_dtypes.bfloat16)


FORWARD, EDGE_IN, COMBINE, TAP_TABLE = tables()
FORWARD = FORWARD.astype(np.float32)
EDGE_HI, EDGE_LO = halves(EDGE_IN)
COMBINE_HI, COMBINE_LO = halves(COMBINE)
TAP_HI, TAP_LO = halves(TAP_TABLE)


def dot(a, b):
    return jnp.dot(a, b, preferred_element_type=F32)


def split(a):
    top = a.astype(B16)
    return top, (a - top.astype(F32)).astype(B16)


def dot3(a, top, low):
    a_top, a_low = split(a)
    return dot(a_top, top) + (dot(a_low, top) + dot(a_top, low))


def place():
    d = lax.axis_index("shot")
    x, z = d // (NZ * NH * NC), d // (NH * NC) % NZ
    return x, z, d // NC % NH, d % NC, lax.axis_index("freq")


def shot_of(x, z, h, c):
    return ((x * NZ + z) * NH + h) * NC + c


def spread_kernel(
    traces, live, bins, cols, owner, surface, filters,
    wave_all, edge_hi_all, edge_lo_all, combine_hi_all, combine_lo_all, tap_hi, tap_lo,
    packed,
    bands, table, wave, edge_hi, edge_lo, combine_hi, combine_lo,
    onehot, factor, cleaned, clean_hi, clean_lo, slots, rows8, bin_col, live_col, filt, f1x,
    r1, m, r2, hown, hin, ag, specp, specr, specall, sa, sb, srot, pred, f1, f1c,
    s1s, s1r, s2s, s2r, hs, hr, gs, gr, bs, br, fs, fr,
    ps, pr, cs, cr, u1s, u1r, u2s, u2r, us, ur, own, consts,
):
    x, z, h, c, f = place()
    mine = x * NC + c

    def dev_p(j):
        p = lax.rem(mine + j, PIECES)
        return p, (shot_of(p // NC, z, h, lax.rem(p, NC)), f)

    def dev_z(j):
        o = lax.rem(z + j, NZ)
        return o, (shot_of(x, o, h, c), f)

    def dev_f(j):
        o = lax.rem(f + j, NQ)
        return o, (shot_of(x, z, h, c), o)

    other_h = (shot_of(x, z, 1 - h, c), f)

    barrier = pltpu.get_barrier_semaphore()

    def greet(dev):
        pl.semaphore_signal(barrier, inc=1, device_id=dev, device_id_type=MESH)

    def each(count, fn):
        def body(j, _):
            fn(j)
            return 0

        lax.fori_loop(1, count, body, 0)

    each(PIECES, lambda j: greet(dev_p(j)[1]))
    each(NZ, lambda j: greet(dev_z(j)[1]))
    each(NQ, lambda j: greet(dev_f(j)[1]))
    greet(other_h)
    pl.semaphore_wait(barrier, PIECES - 1 + NZ - 1 + NQ - 1 + 1)

    def remote(src, dst, send, recv, dev):
        return pltpu.make_async_remote_copy(
            src_ref=src, dst_ref=dst, send_sem=send, recv_sem=recv,
            device_id=dev, device_id_type=MESH,
        )

    def first(k, j, at):
        p, dev = dev_p(j)
        src = surface.at[:, pl.ds(pl.multiple_of(p * (CHUNKS * SUB) + k * SUB, SUB), SUB), :]
        return remote(src, r1.at[k, at(p)], s1s.at[k, p], s1r.at[k, at(p)], dev)

    def second(k, j, at):
        o, dev = dev_z(j)
        return remote(
            m.at[k, :, pl.ds(o * PAIR, PAIR)], r2.at[k, at(o)], s2s.at[k, o], s2r.at[k, at(o)], dev
        )

    def third(k):
        return remote(hown.at[k], hin.at[k], hs.at[k], hr.at[k], other_h)

    def fourth(k, j, at):
        o, dev = dev_z(j)
        return remote(ag.at[k, z], ag.at[k, at(o)], gs.at[k, o], gr.at[k, at(o)], dev)

    def fifth(k, j, at):
        p, dev = dev_p(j)
        return remote(
            pred.at[p, :, k], bands.at[f, :, at(p), k], bs.at[k, p], br.at[k, at(p)], dev
        )

    def sixth(k, j, at):
        o, dev = dev_f(j)
        return remote(
            bands.at[f, :, :, k], bands.at[at(o), :, :, k], fs.at[k, o], fr.at[k, at(o)], dev
        )

    def spec_f(j, at):
        o, dev = dev_f(j)
        return remote(specp.at[o], specr.at[at(o)], ps.at[o], pr.at[at(o)], dev)

    def spec_p(j, at):
        p, dev = dev_p(j)
        return remote(specall.at[mine], specall.at[at(p)], cs.at[p], cr.at[at(p)], dev)

    def filt_p(j, at):
        p, dev = dev_p(j)
        return remote(filt, f1.at[at(p)], u1s.at[p], u1r.at[at(p)], dev)

    def filt_z(j, at):
        o, dev = dev_z(j)
        return remote(f1c, table.at[h, at(o)], u2s.at[o], u2r.at[at(o)], dev)

    def filt_h(at):
        return remote(table.at[h], table.at[at], us, ur, other_h)

    def to_p(p):
        return mine

    def to_z(o):
        return z

    def to_f(o):
        return f

    def here(o):
        return o

    filt[...] = jnp.zeros((SUB, 128), F32)
    filt[0:4, 0:TAPS] = filters[...]
    each(PIECES, lambda j: filt_p(j, to_p).start())

    def start_first(k, _):
        each(PIECES, lambda j: first(k, j, to_p).start())
        return 0

    lax.fori_loop(0, CHUNKS, start_first, 0)

    def own_piece(k):
        src = surface.at[:, pl.ds(pl.multiple_of(mine * (CHUNKS * SUB) + k * SUB, SUB), SUB), :]
        return pltpu.make_async_copy(src, r1.at[k, mine], own.at[k])

    for k in range(CHUNKS):
        own_piece(k).start()

    held = [
        pltpu.make_async_copy(whole.at[f], part, consts.at[i])
        for i, (whole, part) in enumerate((
            (wave_all, wave), (edge_hi_all, edge_hi), (edge_lo_all, edge_lo),
            (combine_hi_all, combine_hi), (combine_lo_all, combine_lo),
        ))
    ]
    for one in held:
        one.start()

    weights = []
    for b in range(STEPS):
        who = owner[b]
        who_p = (who >> 5) * NC + (who & 1)
        who_z = (who >> 2) & (NZ - 1)
        who_h = (who >> 1) & 1
        weights.append(
            [jnp.where(who_p == p, 1.0, 0.0) for p in range(PIECES)]
            + [jnp.where(who_z == o, 1.0, 0.0) for o in range(NZ)]
            + [jnp.where(who_h == h, 1.0, 0.0), jnp.where(who_h == h, 0.0, 1.0)]
        )

    lane_row = lax.broadcasted_iota(I32, (1, R), 1)
    for b in range(STEPS):
        for j in range(POINTS_BLK):
            row = b * POINTS_BLK + j
            onehot[row : row + 1, :] = jnp.where(lane_row == cols[b, j], 1.0, 0.0)
    held[0].wait()
    picked = []
    for s in range(SHOTS):
        pick = onehot[...] * live[s : s + 1, :].astype(F32)
        picked.append(
            jnp.dot(
                pick, traces[s].reshape(R, QUARTER), precision=FULL, preferred_element_type=F32
            )
        )
    part = jnp.dot(
        jnp.concatenate(picked, axis=0), wave[...], precision=FULL, preferred_element_type=F32
    )
    for o in range(NQ):
        specp[o] = part[:, o * LANES : (o + 1) * LANES]
    each(NQ, lambda j: spec_f(j, to_f).start())
    specr[f] = specp[f]

    f1[mine] = filt[...]
    each(PIECES, lambda j: filt_p(j, here).wait_recv())
    for p in range(PIECES):
        for i in range(4):
            f1x[i, p : p + 1, :] = f1[p, i : i + 1, :]
    lined = f1x[0]
    for i in range(1, 4):
        lined = lined + pltpu.roll(f1x[i], i * TAPS, 1)
    f1c[...] = lined
    each(NZ, lambda j: filt_z(j, to_z).start())

    each(NQ, lambda j: spec_f(j, here).wait_recv())
    specall[mine] = specr[0] + specr[1] + specr[2] + specr[3]
    each(PIECES, lambda j: spec_p(j, to_p).start())

    table[h, z] = f1c[...]
    each(NZ, lambda j: filt_z(j, here).wait_recv())
    filt_h(h).start()

    rows8[...] = jnp.zeros((SUB, R), I32)
    rows8[0:SHOTS, :] = bins[...]
    rows8[SHOTS : 2 * SHOTS, :] = live[...]
    turned_rows = rows8[...].T
    for s in range(SHOTS):
        bin_col[s] = turned_rows[:, s : s + 1].reshape(PIECES, CHUNKS, SUB, 1)
        live_col[s] = turned_rows[:, SHOTS + s : SHOTS + s + 1].reshape(PIECES, CHUNKS, SUB, 1)
    for s in range(SHOTS):
        row = bins[s : s + 1, :]
        count = jnp.zeros((1, R), I32)
        for o in range(s + 1):
            hit = jnp.where(turned_rows[:, o : o + 1] == row, 1, 0)
            if o == s:
                before = lax.broadcasted_iota(I32, (R, R), 0) < lax.broadcasted_iota(
                    I32, (R, R), 1
                )
                hit = jnp.where(before, hit, 0)
            count = count + jnp.sum(hit, axis=0, keepdims=True)
        slots[:, s * R : (s + 1) * R] = row * 2 + count

    each(PIECES, lambda j: spec_p(j, here).wait_recv())
    low = lax.broadcasted_iota(jnp.int32, (SHOTS * COLS, LANES), 1) < BAND

    def both(p, _):
        v = specall[p]
        w = pltpu.roll(v, BAND, 1)
        sa[p] = jnp.where(low, v, w)
        sb[p] = jnp.where(low, -w, v)
        return 0

    lax.fori_loop(0, PIECES, both, 0)

    def predict(k):
        each(NZ, lambda j: fourth(k, j, here).wait_recv())
        srot[...] = pltpu.roll(
            ag[k].reshape(NZ * STEPS * PAIR * SUB, LANES), BAND, 1
        ).reshape(NZ, STEPS, PAIR, SUB, LANES)

        def piece(p, _):
            totals = [jnp.zeros((SUB, LANES), F32) for _ in range(SHOTS)]
            for o in range(NZ):
                for b in range(STEPS):
                    for i in range(PAIR):
                        straight, turned = ag[k, o, b, i], srot[o, b, i]
                        for s in range(SHOTS):
                            row = s * COLS + b * POINTS_BLK + o * PAIR + i
                            totals[s] = (
                                totals[s]
                                + sa[p, row : row + 1, :] * straight
                                + sb[p, row : row + 1, :] * turned
                            )
            for s in range(SHOTS):
                pred[p, s, k] = totals[s]
            return 0

        lax.fori_loop(0, PIECES, piece, 0)
        each(PIECES, lambda j: fifth(k, j, to_p).start())
        for s in range(SHOTS):
            bands[f, s, mine, k] = pred[mine, s, k]

    def choose(k):
        own_piece(k).wait()
        each(PIECES, lambda j: first(k, j, here).wait_recv())
        for b in range(STEPS):
            total = jnp.zeros((POINTS_BLK, SUB, LANES), F32)
            for p in range(PIECES):
                total = total + weights[b][p] * r1[k, p]
            m[k, b] = total
        each(NZ, lambda j: second(k, j, to_z).start())
        for b in range(STEPS):
            r2[k, z, b] = m[k, b, pl.ds(z * PAIR, PAIR)]

    def gather(k):
        each(PIECES, lambda j: fifth(k, j, here).wait_recv())
        each(NQ, lambda j: sixth(k, j, to_f).start())

    def across(k):
        each(NZ, lambda j: second(k, j, here).wait_recv())
        for b in range(STEPS):
            total = jnp.zeros((PAIR, SUB, LANES), F32)
            for o in range(NZ):
                total = total + weights[b][PIECES + o] * r2[k, o, b]
            hown[k, b] = total
        third(k).start()

    def share(k):
        third(k).wait_recv()
        for b in range(STEPS):
            ag[k, z, b] = (
                weights[b][PIECES + NZ] * hown[k, b] + weights[b][PIECES + NZ + 1] * hin[k, b]
            )
        each(NZ, lambda j: fourth(k, j, to_z).start())

    tile = SHOTS * PIECES * SUB

    def prepare(k):
        lane = lax.broadcasted_iota(I32, (tile, 128), 1)
        one = bin_col[:, :, k].reshape(tile, 1)
        home = one >> 2
        line = ((home >> 1) & 1) * (NZ * PIECES) + ((home >> 2) & (NZ - 1)) * PIECES
        line = line + (home >> 5) * NC + (home & 1)
        pick = jnp.where(lane == line, 1.0, 0.0).astype(B16)
        all_taps = table[...].reshape(128, 128)
        top, rest = split(all_taps)
        middle, last = split(all_taps - top.astype(F32))
        four = dot(pick, top) + (dot(pick, middle) + dot(pick, last))
        start = (one & 3) * TAPS
        four = jnp.where((lane >= start) & (lane < start + TAPS), four, 0.0)
        factor[k] = dot3(four, tap_hi[...], tap_lo[...])

    def clean(k):
        each(NQ, lambda j: sixth(k, j, here).wait_recv())
        blocks = [bands[o, :, :, k].reshape(tile, LANES) for o in range(NQ)]
        ends = jnp.zeros((tile, 128), F32)
        for o in range(NQ):
            span = slice(o * LANES, (o + 1) * LANES)
            ends = ends + dot3(blocks[o], edge_hi[span, :], edge_lo[span, :])
        blocks.append(ends)
        total = jnp.zeros((tile, QUARTER), F32)
        width = (NQ + 1) * LANES
        for o in range(NQ + 1):
            span = slice(o * LANES, (o + 1) * LANES)
            cross = slice(width + o * LANES, width + (o + 1) * LANES)
            mixed = blocks[o] * factor[k, :, span]
            mixed = mixed + pltpu.roll(blocks[o], BAND, 1) * factor[k, :, cross]
            total = total + dot3(mixed, combine_hi[span, :], combine_lo[span, :])
        alive = live_col[:, :, k].reshape(tile, 1).astype(F32)
        whole = traces[:, :, k].reshape(tile, QUARTER)
        cleaned[:, :, k] = (alive * (whole - total)).reshape(SHOTS, PIECES, SUB, QUARTER)

    def stage(t, lag, fn):
        @pl.when((t >= lag) & (t < lag + CHUNKS))
        def _():
            fn(t - lag)

    for one in held[1:]:
        one.wait()
    filt_h(1 - h).wait_recv()

    def tick(t, _):
        stage(t, 5, clean)
        stage(t, 4, gather)
        stage(t, 3, predict)
        stage(t, 2, share)
        stage(t, 1, across)
        stage(t, 1, prepare)
        stage(t, 0, choose)
        return 0

    lax.fori_loop(0, CHUNKS + 5, tick, 0)

    top, rest = split(cleaned[...].reshape(ROWS, QUARTER))
    clean_hi[...] = top
    clean_lo[...] = rest

    def place_rows(i, _):
        ids = lax.broadcasted_iota(I32, (128, ROWS), 0) + i * 128
        pick = jnp.where(ids == slots[...], 1.0, 0.0).astype(B16)
        packed[pl.ds(pl.multiple_of(i * 128, 128), 128), :] = dot(pick, clean_hi[...]) + dot(
            pick, clean_lo[...]
        )
        return 0

    lax.fori_loop(0, packed.shape[0] // 128, place_rows, 0)

    def finish(k, _):
        each(PIECES, lambda j: first(k, j, to_p).wait_send())
        each(NZ, lambda j: second(k, j, to_z).wait_send())
        third(k).wait_send()
        each(NZ, lambda j: fourth(k, j, to_z).wait_send())
        each(PIECES, lambda j: fifth(k, j, to_p).wait_send())
        each(NQ, lambda j: sixth(k, j, to_f).wait_send())
        return 0

    lax.fori_loop(0, CHUNKS, finish, 0)
    each(NQ, lambda j: spec_f(j, to_f).wait_send())
    each(PIECES, lambda j: spec_p(j, to_p).wait_send())
    each(PIECES, lambda j: filt_p(j, to_p).wait_send())
    each(NZ, lambda j: filt_z(j, to_z).wait_send())
    filt_h(h).wait_send()


def spread(*args):
    dma = pltpu.SemaphoreType.DMA
    v = pltpu.VMEM
    tile = (SUB, LANES)
    vm = pl.BlockSpec(memory_space=pltpu.VMEM)
    sm = pl.BlockSpec(memory_space=pltpu.SMEM)
    hbm = pl.BlockSpec(memory_space=pltpu.HBM)
    small = (STEPS, PAIR, *tile)
    wide = (NQ + 1) * LANES
    return pl.pallas_call(
        spread_kernel,
        out_shape=jax.ShapeDtypeStruct((1024, QUARTER), F32),
        in_specs=[vm, vm, vm, sm, sm, hbm, vm, hbm, hbm, hbm, hbm, hbm, vm, vm],
        out_specs=vm,
        scratch_shapes=[
            v((NQ, SHOTS, PIECES, CHUNKS, *tile), F32),
            v((NH, NZ, PIECES, 128), F32),
            v((QUARTER, NQ * LANES), F32),
            v((NQ * LANES, 128), B16), v((NQ * LANES, 128), B16),
            v((wide, QUARTER), B16), v((wide, QUARTER), B16),
            v((COLS, R), F32),
            v((CHUNKS, SHOTS * PIECES * SUB, 2 * wide), F32),
            v((SHOTS, PIECES, CHUNKS, SUB, QUARTER), F32),
            v((ROWS, QUARTER), B16), v((ROWS, QUARTER), B16),
            v((1, ROWS), I32),
            v((SUB, R), I32),
            v((SHOTS, PIECES, CHUNKS, SUB, 1), I32),
            v((SHOTS, PIECES, CHUNKS, SUB, 1), I32),
            v((SUB, 128), F32),
            v((4, PIECES, 128), F32),
            v((CHUNKS, PIECES, POINTS_BLK, *tile), F32),
            v((CHUNKS, STEPS, POINTS_BLK, *tile), F32),
            v((CHUNKS, NZ, *small), F32),
            v((CHUNKS, *small), F32),
            v((CHUNKS, *small), F32),
            v((CHUNKS, NZ, *small), F32),
            v((NQ, SHOTS * COLS, LANES), F32),
            v((NQ, SHOTS * COLS, LANES), F32),
            v((PIECES, SHOTS * COLS, LANES), F32),
            v((PIECES, SHOTS * COLS, LANES), F32),
            v((PIECES, SHOTS * COLS, LANES), F32),
            v((NZ, *small), F32),
            v((PIECES, SHOTS, CHUNKS, *tile), F32),
            v((PIECES, 8, 128), F32),
            v((PIECES, 128), F32),
            dma((CHUNKS, PIECES)), dma((CHUNKS, PIECES)),
            dma((CHUNKS, NZ)), dma((CHUNKS, NZ)),
            dma((CHUNKS,)), dma((CHUNKS,)),
            dma((CHUNKS, NZ)), dma((CHUNKS, NZ)),
            dma((CHUNKS, PIECES)), dma((CHUNKS, PIECES)),
            dma((CHUNKS, NQ)), dma((CHUNKS, NQ)),
            dma((NQ,)), dma((NQ,)),
            dma((PIECES,)), dma((PIECES,)),
            dma((PIECES,)), dma((PIECES,)),
            dma((NZ,)), dma((NZ,)),
            dma, dma,
            dma((CHUNKS,)),
            dma((5,)),
        ],
        compiler_params=pltpu.CompilerParams(
            collective_id=0, has_side_effects=True, vmem_limit_bytes=48 * 2**20
        ),
    )(*args)


def on_device(traces, live_mask, offset_bin, surface, block_owner, point_column, filters):
    packed = spread(
        traces.reshape(SHOTS, PIECES, CHUNKS, SUB, QUARTER),
        live_mask,
        offset_bin.reshape(SHOTS, R),
        point_column,
        block_owner,
        surface,
        filters,
        *(jnp.asarray(a) for a in (FORWARD, EDGE_HI, EDGE_LO, COMBINE_HI, COMBINE_LO)),
        jnp.asarray(TAP_HI),
        jnp.asarray(TAP_LO),
    )
    packed = packed.reshape(128, 8, QUARTER)
    dealt = lax.all_to_all(packed, "shot", split_axis=0, concat_axis=0, tiled=True)
    dealt = dealt.reshape(128, 4, 2, QUARTER).transpose(1, 0, 2, 3)
    return dealt.reshape(4, 256, QUARTER)


def solution(mesh):
    return jax.shard_map(
        on_device,
        mesh=mesh,
        in_specs=(
            P("shot", None, "freq"),
            P("shot", None),
            P("shot", None, None),
            P("shot", None, "freq"),
            P(),
            P(),
            P("shot", None),
        ),
        out_specs=P("shot", None, "freq"),
        check_vma=False,
    )
```

```python
import jax
import jax.numpy as jnp
import ml_dtypes
import numpy as np
from jax import lax
from jax.experimental import pallas as pl
from jax.experimental.pallas import tpu as pltpu
from jax.sharding import PartitionSpec as P

NT = 1024
NF = 256
TAPS = 31
POINTS_BLK = 16
STEPS = 2
NX, NZ, NH, NC = 4, 8, 2, 2
NQ = 4
BAND = NF // NQ
LANES = 2 * BAND
QUARTER = NT // NQ
R = 256
SHOTS = 3
ROWS = SHOTS * R
PIECES = NX * NC
CHUNKS = 4
SUB = 8
COLS = STEPS * POINTS_BLK
PAIR = POINTS_BLK // NZ
EDGE = (TAPS - 1) // 2
FULL = lax.Precision.HIGHEST
MESH = pl.DeviceIdType.MESH
F32 = jnp.float32
B16 = jnp.bfloat16
I32 = jnp.int32


def tables():
    t = np.arange(NT)
    m = np.arange(NF) + 1
    phase = 2 * np.pi * ((m[:, None] * t[None, :]) % NT) / NT
    real = np.cos(phase).reshape(NQ, BAND, NT)
    imag = -np.sin(phase).reshape(NQ, BAND, NT)
    wave = np.concatenate([real, imag], axis=1).reshape(NQ * LANES, NT)
    forward = wave.T.reshape(NQ, QUARTER, NQ * LANES)
    synth = wave * (2.0 / NT)
    k = np.arange(64)
    u = np.arange(EDGE)
    turn = 2 * np.pi * ((u[:, None] * k[None, :]) % 64) / 64
    short = np.concatenate([np.cos(turn), -np.sin(turn)], axis=1)
    edge = np.zeros((NQ, NQ * LANES, 128))
    edge[0] = synth[:, NT - EDGE :] @ short
    edge[NQ - 1] = synth[:, :EDGE] @ short
    back = np.zeros((NQ, 128, QUARTER))

    def inverse(n):
        a = 2 * np.pi * ((k[:, None] * n[None, :]) % 64) / 64
        return -np.concatenate([np.cos(a), -np.sin(a)], axis=0) / 64

    back[0][:, :EDGE] = inverse(np.arange(2 * EDGE, 3 * EDGE))
    back[NQ - 1][:, QUARTER - EDGE :] = inverse(np.arange(EDGE))
    combine = np.concatenate(
        [synth.reshape(NQ * LANES, NQ, QUARTER).transpose(1, 0, 2), back], axis=1
    )
    i = np.arange(TAPS)
    lag = 2 * np.pi * (((i[:, None] - EDGE) * m[None, :]) % NT) / NT
    c, s = np.cos(lag).reshape(TAPS, NQ, BAND), np.sin(lag).reshape(TAPS, NQ, BAND)
    same = np.concatenate([c, c], axis=2).reshape(TAPS, NQ * LANES)
    cross = np.concatenate([s, -s], axis=2).reshape(TAPS, NQ * LANES)
    lag2 = 2 * np.pi * ((i[:, None] * k[None, :]) % 64) / 64
    same2 = np.concatenate([np.cos(lag2), np.cos(lag2)], axis=1)
    cross2 = np.concatenate([np.sin(lag2), -np.sin(lag2)], axis=1)
    taps = np.concatenate([same, same2, cross, cross2], axis=1)
    taps = np.concatenate([taps] * 4 + [np.zeros((4, taps.shape[1]))], axis=0)
    return forward, edge, combine, taps


def halves(a):
    top = a.astype(ml_dtypes.bfloat16)
    return top, (a - top.astype(np.float64)).astype(ml_dtypes.bfloat16)


FORWARD, EDGE_IN, COMBINE, TAP_TABLE = tables()
FORWARD = FORWARD.astype(np.float32)
EDGE_HI, EDGE_LO = halves(EDGE_IN)
COMBINE_HI, COMBINE_LO = halves(COMBINE)
TAP_HI, TAP_LO = halves(TAP_TABLE)


def dot(a, b):
    return jnp.dot(a, b, preferred_element_type=F32)


def split(a):
    top = a.astype(B16)
    return top, (a - top.astype(F32)).astype(B16)


def dot3(a, top, low):
    a_top, a_low = split(a)
    return dot(a_top, top) + (dot(a_low, top) + dot(a_top, low))


def place():
    d = lax.axis_index("shot")
    x, z = d // (NZ * NH * NC), d // (NH * NC) % NZ
    return x, z, d // NC % NH, d % NC, lax.axis_index("freq")


def shot_of(x, z, h, c):
    return ((x * NZ + z) * NH + h) * NC + c


def spread_kernel(
    traces_in, live_in, bins_in, cols, owner, surface, filters_in,
    wave_all, edge_hi_all, edge_lo_all, combine_hi_all, combine_lo_all, tap_hi_in, tap_lo_in,
    packed,
    traces, live, bins, filters, tap_hi, tap_lo,
    bands, table, wave, edge_hi, edge_lo, combine_hi, combine_lo,
    out_edge_hi, out_edge_lo, out_combine_hi, out_combine_lo, part_out, part_in,
    onehot, factor, cleaned, clean_hi, clean_lo, slots, rows8, bin_col, live_col, filt, f1x,
    r1, m, r2, hown, hin, ag, specp, specr, specall, sa, sb, srot, pred, f1, f1c,
    s1s, s1r, s2s, s2r, hs, hr, gs, gr, bs, br, fs, fr, qs, qr,
    ps, pr, cs, cr, u1s, u1r, u2s, u2r, us, ur, own, consts,
):
    x, z, h, c, f = place()
    mine = x * NC + c

    def dev_p(j):
        p = lax.rem(mine + j, PIECES)
        return p, (shot_of(p // NC, z, h, lax.rem(p, NC)), f)

    def dev_z(j):
        o = lax.rem(z + j, NZ)
        return o, (shot_of(x, o, h, c), f)

    def dev_f(j):
        o = lax.rem(f + j, NQ)
        return o, (shot_of(x, z, h, c), o)

    other_h = (shot_of(x, z, 1 - h, c), f)

    inner = (f == 1) | (f == 2)
    outer = jnp.where(f < 2, 0, NQ - 1)
    inside = jnp.where(f < 2, 1, 2)
    pairs = (
        (filters_in, filters), (live_in, live), (bins_in, bins), (traces_in, traces),
        (wave_all.at[f], wave), (tap_hi_in, tap_hi), (tap_lo_in, tap_lo),
        (edge_hi_all.at[f], edge_hi), (edge_lo_all.at[f], edge_lo),
        (combine_hi_all.at[f], combine_hi), (combine_lo_all.at[f], combine_lo),
        (edge_hi_all.at[outer], out_edge_hi), (edge_lo_all.at[outer], out_edge_lo),
        (combine_hi_all.at[outer], out_combine_hi), (combine_lo_all.at[outer], out_combine_lo),
    )
    held = [pltpu.make_async_copy(a, b, consts.at[i]) for i, (a, b) in enumerate(pairs)]
    for one in held:
        one.start()

    barrier = pltpu.get_barrier_semaphore()

    def greet(dev):
        pl.semaphore_signal(barrier, inc=1, device_id=dev, device_id_type=MESH)

    def each(count, fn):
        def body(j, _):
            fn(j)
            return 0

        lax.fori_loop(1, count, body, 0)

    each(PIECES, lambda j: greet(dev_p(j)[1]))
    each(NZ, lambda j: greet(dev_z(j)[1]))
    each(NQ, lambda j: greet(dev_f(j)[1]))
    greet(other_h)
    pl.semaphore_wait(barrier, PIECES - 1 + NZ - 1 + NQ - 1 + 1)

    def remote(src, dst, send, recv, dev):
        return pltpu.make_async_remote_copy(
            src_ref=src, dst_ref=dst, send_sem=send, recv_sem=recv,
            device_id=dev, device_id_type=MESH,
        )

    def first(k, j, at):
        p, dev = dev_p(j)
        src = surface.at[:, pl.ds(pl.multiple_of(p * (CHUNKS * SUB) + k * SUB, SUB), SUB), :]
        return remote(src, r1.at[k, at(p)], s1s.at[k, p], s1r.at[k, at(p)], dev)

    def second(k, j, at):
        o, dev = dev_z(j)
        return remote(
            m.at[k, :, pl.ds(o * PAIR, PAIR)], r2.at[k, at(o)], s2s.at[k, o], s2r.at[k, at(o)], dev
        )

    def third(k):
        return remote(hown.at[k], hin.at[k], hs.at[k], hr.at[k], other_h)

    def fourth(k, j, at):
        o, dev = dev_z(j)
        return remote(ag.at[k, z], ag.at[k, at(o)], gs.at[k, o], gr.at[k, at(o)], dev)

    def fifth(k, j, at):
        p, dev = dev_p(j)
        return remote(
            pred.at[p, :, k], bands.at[f, :, at(p), k], bs.at[k, p], br.at[k, at(p)], dev
        )

    beside = (shot_of(x, z, h, c), jnp.where(inner, NQ - 1 - f, inside))
    mate = (shot_of(x, z, h, c), NQ - 1 - f)
    edge_dev = (shot_of(x, z, h, c), outer)

    def sixth(k, o):
        return remote(bands.at[f, :, :, k], bands.at[o, :, :, k], fs.at[k, 0], fr.at[k, o], beside)

    def relay(k):
        return remote(
            bands.at[outer, :, :, k], bands.at[outer, :, :, k], fs.at[k, 1], fr.at[k, outer], mate
        )

    def partial_sum(k):
        return remote(part_out.at[k], part_in.at[k], qs.at[k], qr.at[k], edge_dev)

    def spec_f(j, at):
        o, dev = dev_f(j)
        return remote(specp.at[o], specr.at[at(o)], ps.at[o], pr.at[at(o)], dev)

    def spec_p(j, at):
        p, dev = dev_p(j)
        return remote(specall.at[mine], specall.at[at(p)], cs.at[p], cr.at[at(p)], dev)

    def filt_p(j, at):
        p, dev = dev_p(j)
        return remote(filt, f1.at[at(p)], u1s.at[p], u1r.at[at(p)], dev)

    def filt_z(j, at):
        o, dev = dev_z(j)
        return remote(f1c, table.at[h, at(o)], u2s.at[o], u2r.at[at(o)], dev)

    def filt_h(at):
        return remote(table.at[h], table.at[at], us, ur, other_h)

    def to_p(p):
        return mine

    def to_z(o):
        return z

    def to_f(o):
        return f

    def here(o):
        return o

    filt[...] = jnp.zeros((SUB, 128), F32)
    held[0].wait()
    filt[0:4, 0:TAPS] = filters[...]
    each(PIECES, lambda j: filt_p(j, to_p).start())

    def start_first(k, _):
        each(PIECES, lambda j: first(k, j, to_p).start())
        return 0

    lax.fori_loop(0, CHUNKS, start_first, 0)

    def own_piece(k):
        src = surface.at[:, pl.ds(pl.multiple_of(mine * (CHUNKS * SUB) + k * SUB, SUB), SUB), :]
        return pltpu.make_async_copy(src, r1.at[k, mine], own.at[k])

    for k in range(CHUNKS):
        own_piece(k).start()

    weights = []
    for b in range(STEPS):
        who = owner[b]
        who_p = (who >> 5) * NC + (who & 1)
        who_z = (who >> 2) & (NZ - 1)
        who_h = (who >> 1) & 1
        weights.append(
            [jnp.where(who_p == p, 1.0, 0.0) for p in range(PIECES)]
            + [jnp.where(who_z == o, 1.0, 0.0) for o in range(NZ)]
            + [jnp.where(who_h == h, 1.0, 0.0), jnp.where(who_h == h, 0.0, 1.0)]
        )

    lane_row = lax.broadcasted_iota(I32, (1, R), 1)
    for b in range(STEPS):
        for j in range(POINTS_BLK):
            row = b * POINTS_BLK + j
            onehot[row : row + 1, :] = jnp.where(lane_row == cols[b, j], 1.0, 0.0)
    for one in held[1:5]:
        one.wait()
    picked = []
    for s in range(SHOTS):
        pick = onehot[...] * live[s : s + 1, :].astype(F32)
        picked.append(
            jnp.dot(
                pick, traces[s].reshape(R, QUARTER), precision=FULL, preferred_element_type=F32
            )
        )
    part = jnp.dot(
        jnp.concatenate(picked, axis=0), wave[...], precision=FULL, preferred_element_type=F32
    )
    for o in range(NQ):
        specp[o] = part[:, o * LANES : (o + 1) * LANES]
    each(NQ, lambda j: spec_f(j, to_f).start())
    specr[f] = specp[f]
    f1[mine] = filt[...]

    def filters_one():
        each(PIECES, lambda j: filt_p(j, here).wait_recv())
        for p in range(PIECES):
            for i in range(4):
                f1x[i, p : p + 1, :] = f1[p, i : i + 1, :]
        lined = f1x[0]
        for i in range(1, 4):
            lined = lined + pltpu.roll(f1x[i], i * TAPS, 1)
        f1c[...] = lined
        each(NZ, lambda j: filt_z(j, to_z).start())
        table[h, z] = f1c[...]

    def filters_two():
        each(NZ, lambda j: filt_z(j, here).wait_recv())
        filt_h(h).start()

    def filters_three():
        filt_h(1 - h).wait_recv()
        for one in held[5:]:
            one.wait()

    def spectra_one():
        each(NQ, lambda j: spec_f(j, here).wait_recv())
        specall[mine] = specr[0] + specr[1] + specr[2] + specr[3]
        each(PIECES, lambda j: spec_p(j, to_p).start())

    def spectra_two():
        each(PIECES, lambda j: spec_p(j, here).wait_recv())
        low = lax.broadcasted_iota(I32, (SHOTS * COLS, LANES), 1) < BAND

        def both(p, _):
            v = specall[p]
            w = pltpu.roll(v, BAND, 1)
            sa[p] = jnp.where(low, v, w)
            sb[p] = jnp.where(low, -w, v)
            return 0

        lax.fori_loop(0, PIECES, both, 0)

    def ranks():
        rows8[...] = jnp.zeros((SUB, R), I32)
        rows8[0:SHOTS, :] = bins[...].reshape(SHOTS, R)
        rows8[SHOTS : 2 * SHOTS, :] = live[...]
        turned_rows = rows8[...].T
        for s in range(SHOTS):
            bin_col[s] = turned_rows[:, s : s + 1].reshape(PIECES, CHUNKS, SUB, 1)
            live_col[s] = turned_rows[:, SHOTS + s : SHOTS + s + 1].reshape(
                PIECES, CHUNKS, SUB, 1
            )
        for s in range(SHOTS):
            row = bins[s]
            count = jnp.zeros((1, R), I32)
            for o in range(s + 1):
                hit = jnp.where(turned_rows[:, o : o + 1] == row, 1, 0)
                if o == s:
                    before = lax.broadcasted_iota(I32, (R, R), 0) < lax.broadcasted_iota(
                        I32, (R, R), 1
                    )
                    hit = jnp.where(before, hit, 0)
                count = count + jnp.sum(hit, axis=0, keepdims=True)
            slots[:, s * R : (s + 1) * R] = row * 2 + count

    def predict(k):
        each(NZ, lambda j: fourth(k, j, here).wait_recv())
        srot[...] = pltpu.roll(
            ag[k].reshape(NZ * STEPS * PAIR * SUB, LANES), BAND, 1
        ).reshape(NZ, STEPS, PAIR, SUB, LANES)

        def piece(p, _):
            totals = [jnp.zeros((SUB, LANES), F32) for _ in range(SHOTS)]
            for o in range(NZ):
                for b in range(STEPS):
                    for i in range(PAIR):
                        straight, turned = ag[k, o, b, i], srot[o, b, i]
                        for s in range(SHOTS):
                            row = s * COLS + b * POINTS_BLK + o * PAIR + i
                            totals[s] = (
                                totals[s]
                                + sa[p, row : row + 1, :] * straight
                                + sb[p, row : row + 1, :] * turned
                            )
            for s in range(SHOTS):
                pred[p, s, k] = totals[s]
            return 0

        lax.fori_loop(0, PIECES, piece, 0)
        each(PIECES, lambda j: fifth(k, j, to_p).start())
        for s in range(SHOTS):
            bands[f, s, mine, k] = pred[mine, s, k]

    def choose(k):
        own_piece(k).wait()
        each(PIECES, lambda j: first(k, j, here).wait_recv())
        for b in range(STEPS):
            total = jnp.zeros((POINTS_BLK, SUB, LANES), F32)
            for p in range(PIECES):
                total = total + weights[b][p] * r1[k, p]
            m[k, b] = total
        each(NZ, lambda j: second(k, j, to_z).start())
        for b in range(STEPS):
            r2[k, z, b] = m[k, b, pl.ds(z * PAIR, PAIR)]

    def gather(k):
        each(PIECES, lambda j: fifth(k, j, here).wait_recv())
        sixth(k, f).start()

    def across(k):
        each(NZ, lambda j: second(k, j, here).wait_recv())
        for b in range(STEPS):
            total = jnp.zeros((PAIR, SUB, LANES), F32)
            for o in range(NZ):
                total = total + weights[b][PIECES + o] * r2[k, o, b]
            hown[k, b] = total
        third(k).start()

    def share(k):
        third(k).wait_recv()
        for b in range(STEPS):
            ag[k, z, b] = (
                weights[b][PIECES + NZ] * hown[k, b] + weights[b][PIECES + NZ + 1] * hin[k, b]
            )
        each(NZ, lambda j: fourth(k, j, to_z).start())

    tile = SHOTS * PIECES * SUB

    def prepare(k):
        lane = lax.broadcasted_iota(I32, (tile, 128), 1)
        one = bin_col[:, :, k].reshape(tile, 1)
        home = one >> 2
        line = ((home >> 1) & 1) * (NZ * PIECES) + ((home >> 2) & (NZ - 1)) * PIECES
        line = line + (home >> 5) * NC + (home & 1)
        pick = jnp.where(lane == line, 1.0, 0.0).astype(B16)
        all_taps = table[...].reshape(128, 128)
        top, rest = split(all_taps)
        middle, last = split(all_taps - top.astype(F32))
        four = dot(pick, top) + (dot(pick, middle) + dot(pick, last))
        start = (one & 3) * TAPS
        four = jnp.where((lane >= start) & (lane < start + TAPS), four, 0.0)
        answer = dot3(four, tap_hi[...], tap_lo[...])
        for o in range(2 * (NQ + 1)):
            factor[k, o] = answer[:, o * LANES : (o + 1) * LANES]

    def filtered(k, order, e_hi, e_lo, c_hi, c_lo):
        ends = jnp.zeros((tile, 128), F32)
        total = jnp.zeros((tile, QUARTER), F32)

        def mix(block, o, span):
            mixed = block * factor[k, o] + pltpu.roll(block, BAND, 1) * factor[k, NQ + 1 + o]
            return dot3(mixed, c_hi[span, :], c_lo[span, :])

        for o in order:
            span = pl.ds(pl.multiple_of(o * LANES, LANES), LANES)
            block = bands[o, :, :, k].reshape(tile, LANES)
            ends = ends + dot3(block, e_hi[span, :], e_lo[span, :])
            total = total + mix(block, o, span)
        return total + mix(ends, NQ, slice(NQ * LANES, (NQ + 1) * LANES))

    def hand_on(k):
        @pl.when(inner)
        def _():
            sixth(k, outer).wait_recv()
            relay(k).start()

    def reduce_edge(k):
        @pl.when(inner)
        def _():
            sixth(k, NQ - 1 - f).wait_recv()
            sixth(k, NQ - 1 - outer).wait_recv()
            part_out[k] = filtered(
                k, (f, NQ - 1 - f, NQ - 1 - outer),
                out_edge_hi, out_edge_lo, out_combine_hi, out_combine_lo,
            )
            partial_sum(k).start()

    def clean(k):
        def put(total):
            alive = live_col[:, :, k].reshape(tile, 1).astype(F32)
            whole = traces[:, :, k].reshape(tile, QUARTER)
            cleaned[:, :, k] = (alive * (whole - total)).reshape(SHOTS, PIECES, SUB, QUARTER)

        @pl.when(inner)
        def _():
            put(filtered(k, range(NQ), edge_hi, edge_lo, combine_hi, combine_lo))

        @pl.when(~inner)
        def _():
            mine_part = filtered(k, (f,), edge_hi, edge_lo, combine_hi, combine_lo)
            partial_sum(k).wait_recv()
            put(mine_part + part_in[k])

    def stage(t, lag, fn):
        @pl.when((t >= lag) & (t < lag + CHUNKS))
        def _():
            fn(t - lag)

    def tick(t, _):
        stage(t, 0, choose)
        stage(t, 1, across)
        stage(t, 2, share)
        stage(t, 3, predict)
        stage(t, 4, gather)
        stage(t, 5, hand_on)
        stage(t, 6, reduce_edge)
        stage(t, 7, clean)

        @pl.when(t == 0)
        def _():
            filters_one()
            spectra_one()
            ranks()

        @pl.when(t == 1)
        def _():
            filters_two()
            spectra_two()

        @pl.when(t == 2)
        def _():
            filters_three()

        stage(t, 3, prepare)
        return 0

    lax.fori_loop(0, CHUNKS + 7, tick, 0)

    top, rest = split(cleaned[...].reshape(ROWS, QUARTER))
    clean_hi[...] = top
    clean_lo[...] = rest

    def place_rows(i, _):
        ids = lax.broadcasted_iota(I32, (128, ROWS), 0) + i * 128
        pick = jnp.where(ids == slots[...], 1.0, 0.0).astype(B16)
        packed[pl.ds(pl.multiple_of(i * 128, 128), 128), :] = dot(pick, clean_hi[...]) + dot(
            pick, clean_lo[...]
        )
        return 0

    lax.fori_loop(0, packed.shape[0] // 128, place_rows, 0)

    def finish(k, _):
        each(PIECES, lambda j: first(k, j, to_p).wait_send())
        each(NZ, lambda j: second(k, j, to_z).wait_send())
        third(k).wait_send()
        each(NZ, lambda j: fourth(k, j, to_z).wait_send())
        each(PIECES, lambda j: fifth(k, j, to_p).wait_send())
        sixth(k, f).wait_send()

        @pl.when(inner)
        def _():
            relay(k).wait_send()
            partial_sum(k).wait_send()

        return 0

    lax.fori_loop(0, CHUNKS, finish, 0)
    each(NQ, lambda j: spec_f(j, to_f).wait_send())
    each(PIECES, lambda j: spec_p(j, to_p).wait_send())
    each(PIECES, lambda j: filt_p(j, to_p).wait_send())
    each(NZ, lambda j: filt_z(j, to_z).wait_send())
    filt_h(h).wait_send()


def spread(*args):
    dma = pltpu.SemaphoreType.DMA
    v = pltpu.VMEM
    tile = (SUB, LANES)
    vm = pl.BlockSpec(memory_space=pltpu.VMEM)
    sm = pl.BlockSpec(memory_space=pltpu.SMEM)
    hbm = pl.BlockSpec(memory_space=pltpu.HBM)
    small = (STEPS, PAIR, *tile)
    wide = (NQ + 1) * LANES
    return pl.pallas_call(
        spread_kernel,
        out_shape=jax.ShapeDtypeStruct((1024, QUARTER), F32),
        in_specs=[hbm, hbm, hbm, sm, sm] + [hbm] * 9,
        out_specs=vm,
        scratch_shapes=[
            v((SHOTS, PIECES, CHUNKS, SUB, QUARTER), F32),
            v((SHOTS, R), I32), v((SHOTS, 1, R), I32), v((4, TAPS), F32),
            v((128, 2 * wide), B16), v((128, 2 * wide), B16),
            v((NQ, SHOTS, PIECES, CHUNKS, *tile), F32),
            v((NH, NZ, PIECES, 128), F32),
            v((QUARTER, NQ * LANES), F32),
            v((NQ * LANES, 128), B16), v((NQ * LANES, 128), B16),
            v((wide, QUARTER), B16), v((wide, QUARTER), B16),
            v((NQ * LANES, 128), B16), v((NQ * LANES, 128), B16),
            v((wide, QUARTER), B16), v((wide, QUARTER), B16),
            v((CHUNKS, SHOTS * PIECES * SUB, QUARTER), F32),
            v((CHUNKS, SHOTS * PIECES * SUB, QUARTER), F32),
            v((COLS, R), F32),
            v((CHUNKS, 2 * (NQ + 1), SHOTS * PIECES * SUB, LANES), F32),
            v((SHOTS, PIECES, CHUNKS, SUB, QUARTER), F32),
            v((ROWS, QUARTER), B16), v((ROWS, QUARTER), B16),
            v((1, ROWS), I32),
            v((SUB, R), I32),
            v((SHOTS, PIECES, CHUNKS, SUB, 1), I32),
            v((SHOTS, PIECES, CHUNKS, SUB, 1), I32),
            v((SUB, 128), F32),
            v((4, PIECES, 128), F32),
            v((CHUNKS, PIECES, POINTS_BLK, *tile), F32),
            v((CHUNKS, STEPS, POINTS_BLK, *tile), F32),
            v((CHUNKS, NZ, *small), F32),
            v((CHUNKS, *small), F32),
            v((CHUNKS, *small), F32),
            v((CHUNKS, NZ, *small), F32),
            v((NQ, SHOTS * COLS, LANES), F32),
            v((NQ, SHOTS * COLS, LANES), F32),
            v((PIECES, SHOTS * COLS, LANES), F32),
            v((PIECES, SHOTS * COLS, LANES), F32),
            v((PIECES, SHOTS * COLS, LANES), F32),
            v((NZ, *small), F32),
            v((PIECES, SHOTS, CHUNKS, *tile), F32),
            v((PIECES, 8, 128), F32),
            v((PIECES, 128), F32),
            dma((CHUNKS, PIECES)), dma((CHUNKS, PIECES)),
            dma((CHUNKS, NZ)), dma((CHUNKS, NZ)),
            dma((CHUNKS,)), dma((CHUNKS,)),
            dma((CHUNKS, NZ)), dma((CHUNKS, NZ)),
            dma((CHUNKS, PIECES)), dma((CHUNKS, PIECES)),
            dma((CHUNKS, 2)), dma((CHUNKS, NQ)),
            dma((CHUNKS,)), dma((CHUNKS,)),
            dma((NQ,)), dma((NQ,)),
            dma((PIECES,)), dma((PIECES,)),
            dma((PIECES,)), dma((PIECES,)),
            dma((NZ,)), dma((NZ,)),
            dma, dma,
            dma((CHUNKS,)),
            dma((15,)),
        ],
        compiler_params=pltpu.CompilerParams(
            collective_id=0, has_side_effects=True, vmem_limit_bytes=60 * 2**20
        ),
    )(*args)


def on_device(traces, live_mask, offset_bin, surface, block_owner, point_column, filters):
    packed = spread(
        traces.reshape(SHOTS, PIECES, CHUNKS, SUB, QUARTER),
        live_mask,
        offset_bin.reshape(SHOTS, 1, R),
        point_column,
        block_owner,
        surface,
        filters,
        *(jnp.asarray(a) for a in (FORWARD, EDGE_HI, EDGE_LO, COMBINE_HI, COMBINE_LO)),
        jnp.asarray(TAP_HI),
        jnp.asarray(TAP_LO),
    )
    packed = packed.reshape(128, 8, QUARTER)
    dealt = lax.all_to_all(packed, "shot", split_axis=0, concat_axis=0, tiled=True)
    dealt = dealt.reshape(128, 4, 2, QUARTER).transpose(1, 0, 2, 3)
    return dealt.reshape(4, 256, QUARTER)


def solution(mesh):
    return jax.shard_map(
        on_device,
        mesh=mesh,
        in_specs=(
            P("shot", None, "freq"),
            P("shot", None),
            P("shot", None, None),
            P("shot", None, "freq"),
            P(),
            P(),
            P("shot", None),
        ),
        out_specs=P("shot", None, "freq"),
        check_vma=False,
    )
```

```python
import jax
import jax.numpy as jnp
import ml_dtypes
import numpy as np
from jax import lax
from jax.experimental import pallas as pl
from jax.experimental.pallas import tpu as pltpu
from jax.sharding import PartitionSpec as P

NT = 1024
NF = 256
TAPS = 31
POINTS_BLK = 16
STEPS = 2
NX, NZ, NH, NC = 4, 8, 2, 2
NQ = 4
BAND = NF // NQ
LANES = 2 * BAND
QUARTER = NT // NQ
R = 256
SHOTS = 3
SHARDS = NX * NZ * NH * NC
ROWS = SHOTS * R
PIECES = NX * NC
CHUNKS = 4
SUB = 8
COLS = STEPS * POINTS_BLK
PAIR = POINTS_BLK // NZ
EDGE = (TAPS - 1) // 2
FULL = lax.Precision.HIGHEST
MESH = pl.DeviceIdType.MESH
F32 = jnp.float32
B16 = jnp.bfloat16
I32 = jnp.int32


def tables():
    t = np.arange(NT)
    m = np.arange(NF) + 1
    phase = 2 * np.pi * ((m[:, None] * t[None, :]) % NT) / NT
    real = np.cos(phase).reshape(NQ, BAND, NT)
    imag = -np.sin(phase).reshape(NQ, BAND, NT)
    wave = np.concatenate([real, imag], axis=1).reshape(NQ * LANES, NT)
    forward = wave.T.reshape(NQ, QUARTER, NQ * LANES)
    synth = wave * (2.0 / NT)
    k = np.arange(64)
    u = np.arange(EDGE)
    turn = 2 * np.pi * ((u[:, None] * k[None, :]) % 64) / 64
    short = np.concatenate([np.cos(turn), -np.sin(turn)], axis=1)
    edge = np.zeros((NQ, NQ * LANES, 128))
    edge[0] = synth[:, NT - EDGE :] @ short
    edge[NQ - 1] = synth[:, :EDGE] @ short
    back = np.zeros((NQ, 128, QUARTER))

    def inverse(n):
        a = 2 * np.pi * ((k[:, None] * n[None, :]) % 64) / 64
        return -np.concatenate([np.cos(a), -np.sin(a)], axis=0) / 64

    back[0][:, :EDGE] = inverse(np.arange(2 * EDGE, 3 * EDGE))
    back[NQ - 1][:, QUARTER - EDGE :] = inverse(np.arange(EDGE))
    combine = np.concatenate(
        [synth.reshape(NQ * LANES, NQ, QUARTER).transpose(1, 0, 2), back], axis=1
    )
    i = np.arange(TAPS)
    lag = 2 * np.pi * (((i[:, None] - EDGE) * m[None, :]) % NT) / NT
    c, s = np.cos(lag).reshape(TAPS, NQ, BAND), np.sin(lag).reshape(TAPS, NQ, BAND)
    same = np.concatenate([c, c], axis=2).reshape(TAPS, NQ * LANES)
    cross = np.concatenate([s, -s], axis=2).reshape(TAPS, NQ * LANES)
    lag2 = 2 * np.pi * ((i[:, None] * k[None, :]) % 64) / 64
    same2 = np.concatenate([np.cos(lag2), np.cos(lag2)], axis=1)
    cross2 = np.concatenate([np.sin(lag2), -np.sin(lag2)], axis=1)
    taps = np.concatenate([same, same2, cross, cross2], axis=1)
    taps = np.concatenate([taps] * 4 + [np.zeros((4, taps.shape[1]))], axis=0)
    return forward, edge, combine, taps


def halves(a):
    top = a.astype(ml_dtypes.bfloat16)
    return top, (a - top.astype(np.float64)).astype(ml_dtypes.bfloat16)


FORWARD, EDGE_IN, COMBINE, TAP_TABLE = tables()
FORWARD = FORWARD.astype(np.float32)
EDGE_HI, EDGE_LO = halves(EDGE_IN)
COMBINE_HI, COMBINE_LO = halves(COMBINE)
TAP_HI, TAP_LO = halves(TAP_TABLE)


def dot(a, b):
    return jnp.dot(a, b, preferred_element_type=F32)


def split(a):
    top = a.astype(B16)
    return top, (a - top.astype(F32)).astype(B16)


def dot3(a, top, low):
    a_top, a_low = split(a)
    return dot(a_top, top) + (dot(a_low, top) + dot(a_top, low))


def place():
    d = lax.axis_index("shot")
    x, z = d // (NZ * NH * NC), d // (NH * NC) % NZ
    return x, z, d // NC % NH, d % NC, lax.axis_index("freq")


def shot_of(x, z, h, c):
    return ((x * NZ + z) * NH + h) * NC + c


def spread_kernel(
    traces_in, live_in, bins_in, cols, owner, surface, filters_in,
    wave_all, edge_hi_all, edge_lo_all, combine_hi_all, combine_lo_all, tap_hi_in, tap_lo_in,
    arrive,
    packed, traces, live, bins, filters, tap_hi, tap_lo,
    bands, table, wave, edge_hi, edge_lo, combine_hi, combine_lo,
    out_edge_hi, out_edge_lo, out_combine_hi, out_combine_lo, part_out, part_in,
    onehot, factor, cleaned, clean_hi, clean_lo, slots, rows8, bin_col, live_col, filt, f1x,
    r1, m, r2, hown, hin, ag, specp, specr, specall, sa, sb, srot, pred, f1, f1c,
    s1s, s1r, s2s, s2r, hs, hr, gs, gr, bs, br, fs, fr, qs, qr,
    ps, pr, cs, cr, u1s, u1r, u2s, u2r, us, ur, own, consts, ds, dr,
):
    x, z, h, c, f = place()
    mine = x * NC + c

    def dev_p(j):
        p = lax.rem(mine + j, PIECES)
        return p, (shot_of(p // NC, z, h, lax.rem(p, NC)), f)

    def dev_z(j):
        o = lax.rem(z + j, NZ)
        return o, (shot_of(x, o, h, c), f)

    def dev_f(j):
        o = lax.rem(f + j, NQ)
        return o, (shot_of(x, z, h, c), o)

    other_h = (shot_of(x, z, 1 - h, c), f)

    inner = (f == 1) | (f == 2)
    outer = jnp.where(f < 2, 0, NQ - 1)
    inside = jnp.where(f < 2, 1, 2)
    pairs = (
        (filters_in, filters), (live_in, live), (bins_in, bins), (traces_in, traces),
        (wave_all.at[f], wave), (tap_hi_in, tap_hi), (tap_lo_in, tap_lo),
        (edge_hi_all.at[f], edge_hi), (edge_lo_all.at[f], edge_lo),
        (combine_hi_all.at[f], combine_hi), (combine_lo_all.at[f], combine_lo),
        (edge_hi_all.at[outer], out_edge_hi), (edge_lo_all.at[outer], out_edge_lo),
        (combine_hi_all.at[outer], out_combine_hi), (combine_lo_all.at[outer], out_combine_lo),
    )
    held = [pltpu.make_async_copy(a, b, consts.at[i]) for i, (a, b) in enumerate(pairs)]
    for one in held:
        one.start()

    barrier = pltpu.get_barrier_semaphore()

    def greet(dev):
        pl.semaphore_signal(barrier, inc=1, device_id=dev, device_id_type=MESH)

    def each(count, fn):
        def body(j, _):
            fn(j)
            return 0

        lax.fori_loop(1, count, body, 0)

    each(PIECES, lambda j: greet(dev_p(j)[1]))
    each(NZ, lambda j: greet(dev_z(j)[1]))
    each(NQ, lambda j: greet(dev_f(j)[1]))
    greet(other_h)
    pl.semaphore_wait(barrier, PIECES - 1 + NZ - 1 + NQ - 1 + 1)

    def remote(src, dst, send, recv, dev):
        return pltpu.make_async_remote_copy(
            src_ref=src, dst_ref=dst, send_sem=send, recv_sem=recv,
            device_id=dev, device_id_type=MESH,
        )

    def first(k, j, at):
        p, dev = dev_p(j)
        src = surface.at[:, pl.ds(pl.multiple_of(p * (CHUNKS * SUB) + k * SUB, SUB), SUB), :]
        return remote(src, r1.at[k, at(p)], s1s.at[k, p], s1r.at[k, at(p)], dev)

    def second(k, j, at):
        o, dev = dev_z(j)
        return remote(
            m.at[k, :, pl.ds(o * PAIR, PAIR)], r2.at[k, at(o)], s2s.at[k, o], s2r.at[k, at(o)], dev
        )

    def third(k):
        return remote(hown.at[k], hin.at[k], hs.at[k], hr.at[k], other_h)

    def fourth(k, j, at):
        o, dev = dev_z(j)
        return remote(ag.at[k, z], ag.at[k, at(o)], gs.at[k, o], gr.at[k, at(o)], dev)

    def fifth(k, j, at):
        p, dev = dev_p(j)
        return remote(
            pred.at[p, :, k], bands.at[f, :, at(p), k], bs.at[k, p], br.at[k, at(p)], dev
        )

    beside = (shot_of(x, z, h, c), jnp.where(inner, NQ - 1 - f, inside))
    beyond = (shot_of(x, z, h, c), NQ - 1 - inside)
    edge_dev = (shot_of(x, z, h, c), outer)

    def sixth(k, o):
        return remote(bands.at[f, :, :, k], bands.at[o, :, :, k], fs.at[k, 0], fr.at[k, o], beside)

    def farther(k):
        return remote(
            bands.at[f, :, :, k], bands.at[f, :, :, k], fs.at[k, 1], fr.at[k, f], beyond
        )

    def partial_sum(k):
        return remote(part_out.at[k], part_in.at[k], qs.at[k], qr.at[k], edge_dev)

    def spec_f(j, at):
        o, dev = dev_f(j)
        return remote(specp.at[o], specr.at[at(o)], ps.at[o], pr.at[at(o)], dev)

    def spec_p(j, at):
        p, dev = dev_p(j)
        return remote(specall.at[mine], specall.at[at(p)], cs.at[p], cr.at[at(p)], dev)

    def filt_p(j, at):
        p, dev = dev_p(j)
        return remote(filt, f1.at[at(p)], u1s.at[p], u1r.at[at(p)], dev)

    def filt_z(j, at):
        o, dev = dev_z(j)
        return remote(f1c, table.at[h, at(o)], u2s.at[o], u2r.at[at(o)], dev)

    def filt_h(at):
        return remote(table.at[h], table.at[at], us, ur, other_h)

    def to_p(p):
        return mine

    def to_z(o):
        return z

    def to_f(o):
        return f

    def here(o):
        return o

    def start_first(k, _):
        each(PIECES, lambda j: first(k, j, to_p).start())
        return 0

    lax.fori_loop(0, CHUNKS, start_first, 0)

    filt[...] = jnp.zeros((SUB, 128), F32)
    held[0].wait()
    filt[0:4, 0:TAPS] = filters[...]
    each(PIECES, lambda j: filt_p(j, to_p).start())

    def own_piece(k):
        src = surface.at[:, pl.ds(pl.multiple_of(mine * (CHUNKS * SUB) + k * SUB, SUB), SUB), :]
        return pltpu.make_async_copy(src, r1.at[k, mine], own.at[k])

    for k in range(CHUNKS):
        own_piece(k).start()

    weights = []
    for b in range(STEPS):
        who = owner[b]
        who_p = (who >> 5) * NC + (who & 1)
        who_z = (who >> 2) & (NZ - 1)
        who_h = (who >> 1) & 1
        weights.append(
            [jnp.where(who_p == p, 1.0, 0.0) for p in range(PIECES)]
            + [jnp.where(who_z == o, 1.0, 0.0) for o in range(NZ)]
            + [jnp.where(who_h == h, 1.0, 0.0), jnp.where(who_h == h, 0.0, 1.0)]
        )

    lane_row = lax.broadcasted_iota(I32, (1, R), 1)
    for b in range(STEPS):
        for j in range(POINTS_BLK):
            row = b * POINTS_BLK + j
            onehot[row : row + 1, :] = jnp.where(lane_row == cols[b, j], 1.0, 0.0)
    for one in held[1:5]:
        one.wait()
    picked = []
    for s in range(SHOTS):
        pick = onehot[...] * live[s : s + 1, :].astype(F32)
        picked.append(
            jnp.dot(
                pick, traces[s].reshape(R, QUARTER), precision=FULL, preferred_element_type=F32
            )
        )
    part = jnp.dot(
        jnp.concatenate(picked, axis=0), wave[...], precision=FULL, preferred_element_type=F32
    )
    for o in range(NQ):
        specp[o] = part[:, o * LANES : (o + 1) * LANES]
    each(NQ, lambda j: spec_f(j, to_f).start())
    specr[f] = specp[f]
    f1[mine] = filt[...]

    def filters_one():
        each(PIECES, lambda j: filt_p(j, here).wait_recv())
        for p in range(PIECES):
            for i in range(4):
                f1x[i, p : p + 1, :] = f1[p, i : i + 1, :]
        lined = f1x[0]
        for i in range(1, 4):
            lined = lined + pltpu.roll(f1x[i], i * TAPS, 1)
        f1c[...] = lined
        each(NZ, lambda j: filt_z(j, to_z).start())
        table[h, z] = f1c[...]

    def filters_two():
        each(NZ, lambda j: filt_z(j, here).wait_recv())
        filt_h(h).start()

    def filters_three():
        filt_h(1 - h).wait_recv()
        for one in held[5:]:
            one.wait()

    def spectra_one():
        each(NQ, lambda j: spec_f(j, here).wait_recv())
        specall[mine] = specr[0] + specr[1] + specr[2] + specr[3]
        each(PIECES, lambda j: spec_p(j, to_p).start())

    def spectra_two():
        each(PIECES, lambda j: spec_p(j, here).wait_recv())
        low = lax.broadcasted_iota(I32, (SHOTS * COLS, LANES), 1) < BAND

        def both(p, _):
            v = specall[p]
            w = pltpu.roll(v, BAND, 1)
            sa[p] = jnp.where(low, v, w)
            sb[p] = jnp.where(low, -w, v)
            return 0

        lax.fori_loop(0, PIECES, both, 0)

    def ranks():
        rows8[...] = jnp.zeros((SUB, R), I32)
        rows8[0:SHOTS, :] = bins[...].reshape(SHOTS, R)
        rows8[SHOTS : 2 * SHOTS, :] = live[...]
        turned_rows = rows8[...].T
        for s in range(SHOTS):
            bin_col[s] = turned_rows[:, s : s + 1].reshape(PIECES, CHUNKS, SUB, 1)
            live_col[s] = turned_rows[:, SHOTS + s : SHOTS + s + 1].reshape(
                PIECES, CHUNKS, SUB, 1
            )
        for s in range(SHOTS):
            row = bins[s]
            count = jnp.zeros((1, R), I32)
            for o in range(s + 1):
                hit = jnp.where(turned_rows[:, o : o + 1] == row, 1, 0)
                if o == s:
                    before = lax.broadcasted_iota(I32, (R, R), 0) < lax.broadcasted_iota(
                        I32, (R, R), 1
                    )
                    hit = jnp.where(before, hit, 0)
                count = count + jnp.sum(hit, axis=0, keepdims=True)
            slots[:, s * R : (s + 1) * R] = row * 2 + count

    def predict(k):
        each(NZ, lambda j: fourth(k, j, here).wait_recv())
        srot[...] = pltpu.roll(
            ag[k].reshape(NZ * STEPS * PAIR * SUB, LANES), BAND, 1
        ).reshape(NZ, STEPS, PAIR, SUB, LANES)

        def piece(p, _):
            totals = [jnp.zeros((SUB, LANES), F32) for _ in range(SHOTS)]
            for o in range(NZ):
                for b in range(STEPS):
                    for i in range(PAIR):
                        straight, turned = ag[k, o, b, i], srot[o, b, i]
                        for s in range(SHOTS):
                            row = s * COLS + b * POINTS_BLK + o * PAIR + i
                            totals[s] = (
                                totals[s]
                                + sa[p, row : row + 1, :] * straight
                                + sb[p, row : row + 1, :] * turned
                            )
            for s in range(SHOTS):
                pred[p, s, k] = totals[s]
            return 0

        lax.fori_loop(0, PIECES, piece, 0)
        each(PIECES, lambda j: fifth(k, j, to_p).start())
        for s in range(SHOTS):
            bands[f, s, mine, k] = pred[mine, s, k]

    def choose(k):
        own_piece(k).wait()
        each(PIECES, lambda j: first(k, j, here).wait_recv())
        for b in range(STEPS):
            total = jnp.zeros((POINTS_BLK, SUB, LANES), F32)
            for p in range(PIECES):
                total = total + weights[b][p] * r1[k, p]
            m[k, b] = total
        each(NZ, lambda j: second(k, j, to_z).start())
        for b in range(STEPS):
            r2[k, z, b] = m[k, b, pl.ds(z * PAIR, PAIR)]

    def gather(k):
        each(PIECES, lambda j: fifth(k, j, here).wait_recv())
        @pl.when(~inner)
        def _():
            farther(k).start()

        sixth(k, f).start()

    def across(k):
        each(NZ, lambda j: second(k, j, here).wait_recv())
        for b in range(STEPS):
            total = jnp.zeros((PAIR, SUB, LANES), F32)
            for o in range(NZ):
                total = total + weights[b][PIECES + o] * r2[k, o, b]
            hown[k, b] = total
        third(k).start()

    def share(k):
        third(k).wait_recv()
        for b in range(STEPS):
            ag[k, z, b] = (
                weights[b][PIECES + NZ] * hown[k, b] + weights[b][PIECES + NZ + 1] * hin[k, b]
            )
        each(NZ, lambda j: fourth(k, j, to_z).start())

    tile = SHOTS * PIECES * SUB

    def prepare(k):
        lane = lax.broadcasted_iota(I32, (tile, 128), 1)
        one = bin_col[:, :, k].reshape(tile, 1)
        home = one >> 2
        line = ((home >> 1) & 1) * (NZ * PIECES) + ((home >> 2) & (NZ - 1)) * PIECES
        line = line + (home >> 5) * NC + (home & 1)
        pick = jnp.where(lane == line, 1.0, 0.0).astype(B16)
        all_taps = table[...].reshape(128, 128)
        top, rest = split(all_taps)
        middle, last = split(all_taps - top.astype(F32))
        four = dot(pick, top) + (dot(pick, middle) + dot(pick, last))
        start = (one & 3) * TAPS
        four = jnp.where((lane >= start) & (lane < start + TAPS), four, 0.0)
        answer = dot3(four, tap_hi[...], tap_lo[...])
        for o in range(2 * (NQ + 1)):
            factor[k, o] = answer[:, o * LANES : (o + 1) * LANES]

    def filtered(k, order, e_hi, e_lo, c_hi, c_lo):
        ends = jnp.zeros((tile, 128), F32)
        total = jnp.zeros((tile, QUARTER), F32)

        def mix(block, o, span):
            mixed = block * factor[k, o] + pltpu.roll(block, BAND, 1) * factor[k, NQ + 1 + o]
            return dot3(mixed, c_hi[span, :], c_lo[span, :])

        for o in order:
            span = pl.ds(pl.multiple_of(o * LANES, LANES), LANES)
            block = bands[o, :, :, k].reshape(tile, LANES)
            ends = ends + dot3(block, e_hi[span, :], e_lo[span, :])
            total = total + mix(block, o, span)
        return total + mix(ends, NQ, slice(NQ * LANES, (NQ + 1) * LANES))

    def reduce_edge(k):
        @pl.when(inner)
        def _():
            sixth(k, outer).wait_recv()
            sixth(k, NQ - 1 - f).wait_recv()
            sixth(k, NQ - 1 - outer).wait_recv()
            part_out[k] = filtered(
                k, (f, NQ - 1 - f, NQ - 1 - outer),
                out_edge_hi, out_edge_lo, out_combine_hi, out_combine_lo,
            )
            partial_sum(k).start()

    def clean(k):
        def put(total):
            alive = live_col[:, :, k].reshape(tile, 1).astype(F32)
            whole = traces[:, :, k].reshape(tile, QUARTER)
            cleaned[:, :, k] = (alive * (whole - total)).reshape(SHOTS, PIECES, SUB, QUARTER)

        @pl.when(inner)
        def _():
            put(filtered(k, range(NQ), edge_hi, edge_lo, combine_hi, combine_lo))

        @pl.when(~inner)
        def _():
            mine_part = filtered(k, (f,), edge_hi, edge_lo, combine_hi, combine_lo)
            partial_sum(k).wait_recv()
            put(mine_part + part_in[k])

    def stage(t, lag, fn):
        @pl.when((t >= lag) & (t < lag + CHUNKS))
        def _():
            fn(t - lag)

    def tick(t, _):
        stage(t, 0, choose)
        stage(t, 1, across)
        stage(t, 2, share)
        stage(t, 3, predict)
        stage(t, 4, gather)
        stage(t, 5, reduce_edge)
        stage(t, 6, clean)

        @pl.when(t == 0)
        def _():
            filters_one()
            spectra_one()
            ranks()

        @pl.when(t == 1)
        def _():
            filters_two()
            spectra_two()

        @pl.when(t == 2)
        def _():
            filters_three()

        stage(t, 3, prepare)
        return 0

    lax.fori_loop(0, CHUNKS + 6, tick, 0)

    top, rest = split(cleaned[...].reshape(ROWS, QUARTER))
    clean_hi[...] = top
    clean_lo[...] = rest

    me = shot_of(x, z, h, c)
    group = 128 // SUB

    def deal(t):
        return remote(packed.at[t], arrive.at[me], ds, dr, (t, f))

    def place_rows(i, _):
        g = lax.rem(me // group + i, SHARDS // group)
        ids = lax.broadcasted_iota(I32, (128, ROWS), 0) + g * 128
        pick = jnp.where(ids == slots[...], 1.0, 0.0).astype(B16)
        block = dot(pick, clean_hi[...]) + dot(pick, clean_lo[...])
        packed[pl.ds(g * group, group)] = block.reshape(group, SUB, QUARTER)

        def send(j, _):
            t = g * group + lax.rem(me + j, group)

            @pl.when(t != me)
            def _():
                deal(t).start()

            return 0

        lax.fori_loop(0, group, send, 0)
        return 0

    lax.fori_loop(0, SHARDS // group, place_rows, 0)
    arrive[me] = packed[me]

    def finish(k, _):
        each(PIECES, lambda j: first(k, j, to_p).wait_send())
        each(NZ, lambda j: second(k, j, to_z).wait_send())
        third(k).wait_send()
        each(NZ, lambda j: fourth(k, j, to_z).wait_send())
        each(PIECES, lambda j: fifth(k, j, to_p).wait_send())
        sixth(k, f).wait_send()

        @pl.when(~inner)
        def _():
            farther(k).wait_send()

        @pl.when(inner)
        def _():
            partial_sum(k).wait_send()

        return 0

    lax.fori_loop(0, CHUNKS, finish, 0)
    each(NQ, lambda j: spec_f(j, to_f).wait_send())
    each(PIECES, lambda j: spec_p(j, to_p).wait_send())
    each(PIECES, lambda j: filt_p(j, to_p).wait_send())
    each(NZ, lambda j: filt_z(j, to_z).wait_send())
    filt_h(h).wait_send()
    others = pl.ds(0, SHARDS - 1)
    pltpu.make_async_copy(packed.at[others], packed.at[others], ds).wait()
    pltpu.make_async_copy(arrive.at[others], arrive.at[others], dr).wait()


def spread(*args):
    dma = pltpu.SemaphoreType.DMA
    v = pltpu.VMEM
    tile = (SUB, LANES)
    vm = pl.BlockSpec(memory_space=pltpu.VMEM)
    sm = pl.BlockSpec(memory_space=pltpu.SMEM)
    hbm = pl.BlockSpec(memory_space=pltpu.HBM)
    small = (STEPS, PAIR, *tile)
    wide = (NQ + 1) * LANES
    return pl.pallas_call(
        spread_kernel,
        out_shape=jax.ShapeDtypeStruct((SHARDS, SUB, QUARTER), F32),
        in_specs=[hbm, hbm, hbm, sm, sm] + [hbm] * 9,
        out_specs=vm,
        scratch_shapes=[
            v((SHARDS, SUB, QUARTER), F32),
            v((SHOTS, PIECES, CHUNKS, SUB, QUARTER), F32),
            v((SHOTS, R), I32), v((SHOTS, 1, R), I32), v((4, TAPS), F32),
            v((128, 2 * wide), B16), v((128, 2 * wide), B16),
            v((NQ, SHOTS, PIECES, CHUNKS, *tile), F32),
            v((NH, NZ, PIECES, 128), F32),
            v((QUARTER, NQ * LANES), F32),
            v((NQ * LANES, 128), B16), v((NQ * LANES, 128), B16),
            v((wide, QUARTER), B16), v((wide, QUARTER), B16),
            v((NQ * LANES, 128), B16), v((NQ * LANES, 128), B16),
            v((wide, QUARTER), B16), v((wide, QUARTER), B16),
            v((CHUNKS, SHOTS * PIECES * SUB, QUARTER), F32),
            v((CHUNKS, SHOTS * PIECES * SUB, QUARTER), F32),
            v((COLS, R), F32),
            v((CHUNKS, 2 * (NQ + 1), SHOTS * PIECES * SUB, LANES), F32),
            v((SHOTS, PIECES, CHUNKS, SUB, QUARTER), F32),
            v((ROWS, QUARTER), B16), v((ROWS, QUARTER), B16),
            v((1, ROWS), I32),
            v((SUB, R), I32),
            v((SHOTS, PIECES, CHUNKS, SUB, 1), I32),
            v((SHOTS, PIECES, CHUNKS, SUB, 1), I32),
            v((SUB, 128), F32),
            v((4, PIECES, 128), F32),
            v((CHUNKS, PIECES, POINTS_BLK, *tile), F32),
            v((CHUNKS, STEPS, POINTS_BLK, *tile), F32),
            v((CHUNKS, NZ, *small), F32),
            v((CHUNKS, *small), F32),
            v((CHUNKS, *small), F32),
            v((CHUNKS, NZ, *small), F32),
            v((NQ, SHOTS * COLS, LANES), F32),
            v((NQ, SHOTS * COLS, LANES), F32),
            v((PIECES, SHOTS * COLS, LANES), F32),
            v((PIECES, SHOTS * COLS, LANES), F32),
            v((PIECES, SHOTS * COLS, LANES), F32),
            v((NZ, *small), F32),
            v((PIECES, SHOTS, CHUNKS, *tile), F32),
            v((PIECES, 8, 128), F32),
            v((PIECES, 128), F32),
            dma((CHUNKS, PIECES)), dma((CHUNKS, PIECES)),
            dma((CHUNKS, NZ)), dma((CHUNKS, NZ)),
            dma((CHUNKS,)), dma((CHUNKS,)),
            dma((CHUNKS, NZ)), dma((CHUNKS, NZ)),
            dma((CHUNKS, PIECES)), dma((CHUNKS, PIECES)),
            dma((CHUNKS, 2)), dma((CHUNKS, NQ)),
            dma((CHUNKS,)), dma((CHUNKS,)),
            dma((NQ,)), dma((NQ,)),
            dma((PIECES,)), dma((PIECES,)),
            dma((PIECES,)), dma((PIECES,)),
            dma((NZ,)), dma((NZ,)),
            dma, dma,
            dma((CHUNKS,)),
            dma((15,)),
            dma, dma,
        ],
        compiler_params=pltpu.CompilerParams(
            collective_id=0, has_side_effects=True, vmem_limit_bytes=60 * 2**20
        ),
    )(*args)


def on_device(traces, live_mask, offset_bin, surface, block_owner, point_column, filters):
    dealt = spread(
        traces.reshape(SHOTS, PIECES, CHUNKS, SUB, QUARTER),
        live_mask,
        offset_bin.reshape(SHOTS, 1, R),
        point_column,
        block_owner,
        surface,
        filters,
        *(jnp.asarray(a) for a in (FORWARD, EDGE_HI, EDGE_LO, COMBINE_HI, COMBINE_LO)),
        jnp.asarray(TAP_HI),
        jnp.asarray(TAP_LO),
    )
    dealt = dealt.reshape(SHARDS, 4, 2, QUARTER).transpose(1, 0, 2, 3)
    return dealt.reshape(4, 256, QUARTER)


def solution(mesh):
    return jax.shard_map(
        on_device,
        mesh=mesh,
        in_specs=(
            P("shot", None, "freq"),
            P("shot", None),
            P("shot", None, None),
            P("shot", None, "freq"),
            P(),
            P(),
            P("shot", None),
        ),
        out_specs=P("shot", None, "freq"),
        check_vma=False,
    )
```

```python
import jax
import jax.numpy as jnp
import ml_dtypes
import numpy as np
from jax import lax
from jax.experimental import pallas as pl
from jax.experimental.pallas import tpu as pltpu
from jax.sharding import PartitionSpec as P

NT = 1024
NF = 256
TAPS = 31
POINTS_BLK = 16
STEPS = 2
NX, NZ, NH, NC = 4, 8, 2, 2
NQ = 4
BAND = NF // NQ
LANES = 2 * BAND
QUARTER = NT // NQ
R = 256
SHOTS = 3
MOST = 2
SHARDS = NX * NZ * NH * NC
ROWS = SHOTS * R
PIECES = NX * NC
CHUNKS = 4
AHEAD = 2
SUB = 8
COLS = STEPS * POINTS_BLK
PAIR = POINTS_BLK // NZ
EDGE = (TAPS - 1) // 2
FULL = lax.Precision.HIGHEST
MESH = pl.DeviceIdType.MESH
F32 = jnp.float32
B16 = jnp.bfloat16
I32 = jnp.int32


def tables():
    t = np.arange(NT)
    m = np.arange(NF) + 1
    phase = 2 * np.pi * ((m[:, None] * t[None, :]) % NT) / NT
    real = np.cos(phase).reshape(NQ, BAND, NT)
    imag = -np.sin(phase).reshape(NQ, BAND, NT)
    wave = np.concatenate([real, imag], axis=1).reshape(NQ * LANES, NT)
    forward = wave.T.reshape(NQ, QUARTER, NQ * LANES)
    synth = wave * (2.0 / NT)
    k = np.arange(64)
    u = np.arange(EDGE)
    turn = 2 * np.pi * ((u[:, None] * k[None, :]) % 64) / 64
    short = np.concatenate([np.cos(turn), -np.sin(turn)], axis=1)
    edge = np.zeros((NQ, NQ * LANES, 128))
    edge[0] = synth[:, NT - EDGE :] @ short
    edge[NQ - 1] = synth[:, :EDGE] @ short
    back = np.zeros((NQ, 128, QUARTER))

    def inverse(n):
        a = 2 * np.pi * ((k[:, None] * n[None, :]) % 64) / 64
        return -np.concatenate([np.cos(a), -np.sin(a)], axis=0) / 64

    back[0][:, :EDGE] = inverse(np.arange(2 * EDGE, 3 * EDGE))
    back[NQ - 1][:, QUARTER - EDGE :] = inverse(np.arange(EDGE))
    combine = np.concatenate(
        [synth.reshape(NQ * LANES, NQ, QUARTER).transpose(1, 0, 2), back], axis=1
    )
    i = np.arange(TAPS)
    lag = 2 * np.pi * (((i[:, None] - EDGE) * m[None, :]) % NT) / NT
    c, s = np.cos(lag).reshape(TAPS, NQ, BAND), np.sin(lag).reshape(TAPS, NQ, BAND)
    same = np.concatenate([c, c], axis=2).reshape(TAPS, NQ * LANES)
    cross = np.concatenate([s, -s], axis=2).reshape(TAPS, NQ * LANES)
    lag2 = 2 * np.pi * ((i[:, None] * k[None, :]) % 64) / 64
    same2 = np.concatenate([np.cos(lag2), np.cos(lag2)], axis=1)
    cross2 = np.concatenate([np.sin(lag2), -np.sin(lag2)], axis=1)
    taps = np.concatenate([same, same2, cross, cross2], axis=1)
    taps = np.concatenate([taps] * 4 + [np.zeros((4, taps.shape[1]))], axis=0)
    return forward, edge, combine, taps


def halves(a):
    top = a.astype(ml_dtypes.bfloat16)
    return top, (a - top.astype(np.float64)).astype(ml_dtypes.bfloat16)


FORWARD, EDGE_IN, COMBINE, TAP_TABLE = tables()
FORWARD = FORWARD.astype(np.float32)
EDGE_HI, EDGE_LO = halves(EDGE_IN)
COMBINE_HI, COMBINE_LO = halves(COMBINE)
TAP_HI, TAP_LO = halves(TAP_TABLE)


def dot(a, b):
    return jnp.dot(a, b, preferred_element_type=F32)


def split(a):
    top = a.astype(B16)
    return top, (a - top.astype(F32)).astype(B16)


def dot3(a, top, low):
    a_top, a_low = split(a)
    return dot(a_top, top) + (dot(a_low, top) + dot(a_top, low))


def place():
    d = lax.axis_index("shot")
    x, z = d // (NZ * NH * NC), d // (NH * NC) % NZ
    return x, z, d // NC % NH, d % NC, lax.axis_index("freq")


def shot_of(x, z, h, c):
    return ((x * NZ + z) * NH + h) * NC + c


def spread_kernel(
    traces_in, live_in, bins_in, cols, owner, surface, filters_in,
    wave_all, edge_hi_all, edge_lo_all, combine_hi_all, combine_lo_all, tap_hi_in, tap_lo_in,
    sorted_rows,
    arrive, packed, traces, live, bins, filters, tap_hi, tap_lo,
    bands, table, wave, edge_hi, edge_lo, combine_hi, combine_lo,
    out_edge_hi, out_edge_lo, out_combine_hi, out_combine_lo, part_out, part_in,
    onehot, factor, cleaned, clean_hi, clean_lo, slots, rows8, bin_col, live_col, filt, f1x,
    r1, m, r2, hown, hin, ag, specp, specr, specall, sa, sb, srot, pred, f1, f1c,
    s1s, s1r, s2s, s2r, hs, hr, gs, gr, bs, br, fs, fr, qs, qr,
    ps, pr, cs, cr, u1s, u1r, u2s, u2r, us, ur, own, consts, ds, dr,
):
    x, z, h, c, f = place()
    mine = x * NC + c

    def dev_p(j):
        p = lax.rem(mine + j, PIECES)
        return p, (shot_of(p // NC, z, h, lax.rem(p, NC)), f)

    def dev_z(j):
        o = lax.rem(z + j, NZ)
        return o, (shot_of(x, o, h, c), f)

    def dev_f(j):
        o = lax.rem(f + j, NQ)
        return o, (shot_of(x, z, h, c), o)

    other_h = (shot_of(x, z, 1 - h, c), f)

    inner = (f == 1) | (f == 2)
    outer = jnp.where(f < 2, 0, NQ - 1)
    inside = jnp.where(f < 2, 1, 2)
    pairs = (
        (filters_in, filters), (live_in, live), (bins_in, bins), (traces_in, traces),
        (wave_all.at[f], wave), (tap_hi_in, tap_hi), (tap_lo_in, tap_lo),
        (edge_hi_all.at[f], edge_hi), (edge_lo_all.at[f], edge_lo),
        (combine_hi_all.at[f], combine_hi), (combine_lo_all.at[f], combine_lo),
        (edge_hi_all.at[outer], out_edge_hi), (edge_lo_all.at[outer], out_edge_lo),
        (combine_hi_all.at[outer], out_combine_hi), (combine_lo_all.at[outer], out_combine_lo),
    )
    held = [pltpu.make_async_copy(a, b, consts.at[i]) for i, (a, b) in enumerate(pairs)]
    for one in held:
        one.start()

    barrier = pltpu.get_barrier_semaphore()

    def greet(dev):
        pl.semaphore_signal(barrier, inc=1, device_id=dev, device_id_type=MESH)

    def each(count, fn):
        def body(j, _):
            fn(j)
            return 0

        lax.fori_loop(1, count, body, 0)

    each(PIECES, lambda j: greet(dev_p(j)[1]))
    each(NZ, lambda j: greet(dev_z(j)[1]))
    each(NQ, lambda j: greet(dev_f(j)[1]))
    greet(other_h)
    pl.semaphore_wait(barrier, PIECES - 1 + NZ - 1 + NQ - 1 + 1)

    def remote(src, dst, send, recv, dev):
        return pltpu.make_async_remote_copy(
            src_ref=src, dst_ref=dst, send_sem=send, recv_sem=recv,
            device_id=dev, device_id_type=MESH,
        )

    def first(k, j, at):
        p, dev = dev_p(j)
        src = surface.at[:, pl.ds(pl.multiple_of(p * (CHUNKS * SUB) + k * SUB, SUB), SUB), :]
        return remote(src, r1.at[k, at(p)], s1s.at[k, p], s1r.at[k, at(p)], dev)

    def second(k, j, at):
        o, dev = dev_z(j)
        return remote(
            m.at[k, :, pl.ds(o * PAIR, PAIR)], r2.at[k, at(o)], s2s.at[k, o], s2r.at[k, at(o)], dev
        )

    def third(k):
        return remote(hown.at[k], hin.at[k], hs.at[k], hr.at[k], other_h)

    def fourth(k, j, at):
        o, dev = dev_z(j)
        return remote(ag.at[k, z], ag.at[k, at(o)], gs.at[k, o], gr.at[k, at(o)], dev)

    def fifth(k, j, at):
        p, dev = dev_p(j)
        return remote(
            pred.at[p, :, k], bands.at[f, :, at(p), k], bs.at[k, p], br.at[k, at(p)], dev
        )

    beside = (shot_of(x, z, h, c), jnp.where(inner, NQ - 1 - f, inside))
    beyond = (shot_of(x, z, h, c), NQ - 1 - inside)
    edge_dev = (shot_of(x, z, h, c), outer)

    def sixth(k, o):
        return remote(bands.at[f, :, :, k], bands.at[o, :, :, k], fs.at[k, 0], fr.at[k, o], beside)

    def farther(k):
        return remote(
            bands.at[f, :, :, k], bands.at[f, :, :, k], fs.at[k, 1], fr.at[k, f], beyond
        )

    def partial_sum(k):
        return remote(part_out.at[k], part_in.at[k], qs.at[k], qr.at[k], edge_dev)

    def spec_f(j, at):
        o, dev = dev_f(j)
        return remote(specp.at[o], specr.at[at(o)], ps.at[o], pr.at[at(o)], dev)

    def spec_p(j, at):
        p, dev = dev_p(j)
        return remote(specall.at[mine], specall.at[at(p)], cs.at[p], cr.at[at(p)], dev)

    def filt_p(j, at):
        p, dev = dev_p(j)
        return remote(filt, f1.at[at(p)], u1s.at[p], u1r.at[at(p)], dev)

    def filt_z(j, at):
        o, dev = dev_z(j)
        return remote(f1c, table.at[h, at(o)], u2s.at[o], u2r.at[at(o)], dev)

    def filt_h(at):
        return remote(table.at[h], table.at[at], us, ur, other_h)

    def to_p(p):
        return mine

    def to_z(o):
        return z

    def to_f(o):
        return f

    def here(o):
        return o

    def start_first(k, _):
        each(PIECES, lambda j: first(k, j, to_p).start())
        return 0

    filt[...] = jnp.zeros((SUB, 128), F32)
    held[0].wait()
    filt[0:4, 0:TAPS] = filters[...]
    each(PIECES, lambda j: filt_p(j, to_p).start())

    lax.fori_loop(0, AHEAD, start_first, 0)

    def own_piece(k):
        src = surface.at[:, pl.ds(pl.multiple_of(mine * (CHUNKS * SUB) + k * SUB, SUB), SUB), :]
        return pltpu.make_async_copy(src, r1.at[k, mine], own.at[k])

    for k in range(CHUNKS):
        own_piece(k).start()

    weights = []
    for b in range(STEPS):
        who = owner[b]
        who_p = (who >> 5) * NC + (who & 1)
        who_z = (who >> 2) & (NZ - 1)
        who_h = (who >> 1) & 1
        weights.append(
            [jnp.where(who_p == p, 1.0, 0.0) for p in range(PIECES)]
            + [jnp.where(who_z == o, 1.0, 0.0) for o in range(NZ)]
            + [jnp.where(who_h == h, 1.0, 0.0), jnp.where(who_h == h, 0.0, 1.0)]
        )

    lane_row = lax.broadcasted_iota(I32, (1, R), 1)
    for b in range(STEPS):
        for j in range(POINTS_BLK):
            row = b * POINTS_BLK + j
            onehot[row : row + 1, :] = jnp.where(lane_row == cols[b, j], 1.0, 0.0)
    for one in held[1:5]:
        one.wait()
    picked = []
    for s in range(SHOTS):
        pick = onehot[...] * live[s : s + 1, :].astype(F32)
        picked.append(
            jnp.dot(
                pick, traces[s].reshape(R, QUARTER), precision=FULL, preferred_element_type=F32
            )
        )
    part = jnp.dot(
        jnp.concatenate(picked, axis=0), wave[...], precision=FULL, preferred_element_type=F32
    )
    for o in range(NQ):
        specp[o] = part[:, o * LANES : (o + 1) * LANES]
    each(NQ, lambda j: spec_f(j, to_f).start())
    specr[f] = specp[f]
    f1[mine] = filt[...]

    def filters_one():
        each(PIECES, lambda j: filt_p(j, here).wait_recv())
        for p in range(PIECES):
            for i in range(4):
                f1x[i, p : p + 1, :] = f1[p, i : i + 1, :]
        lined = f1x[0]
        for i in range(1, 4):
            lined = lined + pltpu.roll(f1x[i], i * TAPS, 1)
        f1c[...] = lined
        each(NZ, lambda j: filt_z(j, to_z).start())
        table[h, z] = f1c[...]

    def filters_two():
        each(NZ, lambda j: filt_z(j, here).wait_recv())
        filt_h(h).start()

    def filters_three():
        filt_h(1 - h).wait_recv()
        for one in held[5:]:
            one.wait()

    def spectra_one():
        each(NQ, lambda j: spec_f(j, here).wait_recv())
        specall[mine] = specr[0] + specr[1] + specr[2] + specr[3]
        each(PIECES, lambda j: spec_p(j, to_p).start())

    def spectra_two():
        each(PIECES, lambda j: spec_p(j, here).wait_recv())
        low = lax.broadcasted_iota(I32, (SHOTS * COLS, LANES), 1) < BAND

        def both(p, _):
            v = specall[p]
            w = pltpu.roll(v, BAND, 1)
            sa[p] = jnp.where(low, v, w)
            sb[p] = jnp.where(low, -w, v)
            return 0

        lax.fori_loop(0, PIECES, both, 0)

    def ranks():
        rows8[...] = jnp.zeros((SUB, R), I32)
        rows8[0:SHOTS, :] = bins[...].reshape(SHOTS, R)
        rows8[SHOTS : 2 * SHOTS, :] = live[...]
        turned_rows = rows8[...].T
        for s in range(SHOTS):
            bin_col[s] = turned_rows[:, s : s + 1].reshape(PIECES, CHUNKS, SUB, 1)
            live_col[s] = turned_rows[:, SHOTS + s : SHOTS + s + 1].reshape(
                PIECES, CHUNKS, SUB, 1
            )
        for s in range(SHOTS):
            row = bins[s]
            count = jnp.zeros((1, R), I32)
            for o in range(s + 1):
                hit = jnp.where(turned_rows[:, o : o + 1] == row, 1, 0)
                if o == s:
                    before = lax.broadcasted_iota(I32, (R, R), 0) < lax.broadcasted_iota(
                        I32, (R, R), 1
                    )
                    hit = jnp.where(before, hit, 0)
                count = count + jnp.sum(hit, axis=0, keepdims=True)
            slots[:, s * R : (s + 1) * R] = row * 2 + count

    def predict(k):
        each(NZ, lambda j: fourth(k, j, here).wait_recv())
        srot[...] = pltpu.roll(
            ag[k].reshape(NZ * STEPS * PAIR * SUB, LANES), BAND, 1
        ).reshape(NZ, STEPS, PAIR, SUB, LANES)

        def piece(p, _):
            totals = [jnp.zeros((SUB, LANES), F32) for _ in range(SHOTS)]
            for o in range(NZ):
                for b in range(STEPS):
                    for i in range(PAIR):
                        straight, turned = ag[k, o, b, i], srot[o, b, i]
                        for s in range(SHOTS):
                            row = s * COLS + b * POINTS_BLK + o * PAIR + i
                            totals[s] = (
                                totals[s]
                                + sa[p, row : row + 1, :] * straight
                                + sb[p, row : row + 1, :] * turned
                            )
            for s in range(SHOTS):
                pred[p, s, k] = totals[s]
            return 0

        lax.fori_loop(0, PIECES, piece, 0)
        each(PIECES, lambda j: fifth(k, j, to_p).start())
        for s in range(SHOTS):
            bands[f, s, mine, k] = pred[mine, s, k]

    def choose(k):
        own_piece(k).wait()
        each(PIECES, lambda j: first(k, j, here).wait_recv())
        for b in range(STEPS):
            total = jnp.zeros((POINTS_BLK, SUB, LANES), F32)
            for p in range(PIECES):
                total = total + weights[b][p] * r1[k, p]
            m[k, b] = total
        each(NZ, lambda j: second(k, j, to_z).start())
        for b in range(STEPS):
            r2[k, z, b] = m[k, b, pl.ds(z * PAIR, PAIR)]

    def gather(k):
        each(PIECES, lambda j: fifth(k, j, here).wait_recv())
        @pl.when(~inner)
        def _():
            farther(k).start()

        sixth(k, f).start()

    def across(k):
        each(NZ, lambda j: second(k, j, here).wait_recv())
        for b in range(STEPS):
            total = jnp.zeros((PAIR, SUB, LANES), F32)
            for o in range(NZ):
                total = total + weights[b][PIECES + o] * r2[k, o, b]
            hown[k, b] = total
        third(k).start()

    def share(k):
        third(k).wait_recv()
        for b in range(STEPS):
            ag[k, z, b] = (
                weights[b][PIECES + NZ] * hown[k, b] + weights[b][PIECES + NZ + 1] * hin[k, b]
            )
        each(NZ, lambda j: fourth(k, j, to_z).start())

    tile = SHOTS * PIECES * SUB

    def prepare(k):
        lane = lax.broadcasted_iota(I32, (tile, 128), 1)
        one = bin_col[:, :, k].reshape(tile, 1)
        home = one >> 2
        line = ((home >> 1) & 1) * (NZ * PIECES) + ((home >> 2) & (NZ - 1)) * PIECES
        line = line + (home >> 5) * NC + (home & 1)
        pick = jnp.where(lane == line, 1.0, 0.0).astype(B16)
        all_taps = table[...].reshape(128, 128)
        top, rest = split(all_taps)
        middle, last = split(all_taps - top.astype(F32))
        four = dot(pick, top) + (dot(pick, middle) + dot(pick, last))
        start = (one & 3) * TAPS
        four = jnp.where((lane >= start) & (lane < start + TAPS), four, 0.0)
        answer = dot3(four, tap_hi[...], tap_lo[...])
        for o in range(2 * (NQ + 1)):
            factor[k, o] = answer[:, o * LANES : (o + 1) * LANES]

    def filtered(k, order, e_hi, e_lo, c_hi, c_lo):
        ends = jnp.zeros((tile, 128), F32)
        total = jnp.zeros((tile, QUARTER), F32)

        def mix(block, o, span):
            mixed = block * factor[k, o] + pltpu.roll(block, BAND, 1) * factor[k, NQ + 1 + o]
            return dot3(mixed, c_hi[span, :], c_lo[span, :])

        for o in order:
            span = pl.ds(pl.multiple_of(o * LANES, LANES), LANES)
            block = bands[o, :, :, k].reshape(tile, LANES)
            ends = ends + dot3(block, e_hi[span, :], e_lo[span, :])
            total = total + mix(block, o, span)
        return total + mix(ends, NQ, slice(NQ * LANES, (NQ + 1) * LANES))

    def reduce_edge(k):
        @pl.when(inner)
        def _():
            sixth(k, outer).wait_recv()
            sixth(k, NQ - 1 - f).wait_recv()
            sixth(k, NQ - 1 - outer).wait_recv()
            part_out[k] = filtered(
                k, (f, NQ - 1 - f, NQ - 1 - outer),
                out_edge_hi, out_edge_lo, out_combine_hi, out_combine_lo,
            )
            partial_sum(k).start()

    def clean(k):
        def put(total):
            alive = live_col[:, :, k].reshape(tile, 1).astype(F32)
            whole = traces[:, :, k].reshape(tile, QUARTER)
            cleaned[:, :, k] = (alive * (whole - total)).reshape(SHOTS, PIECES, SUB, QUARTER)

        @pl.when(inner)
        def _():
            put(filtered(k, range(NQ), edge_hi, edge_lo, combine_hi, combine_lo))

        @pl.when(~inner)
        def _():
            mine_part = filtered(k, (f,), edge_hi, edge_lo, combine_hi, combine_lo)
            partial_sum(k).wait_recv()
            put(mine_part + part_in[k])

    def stage(t, lag, fn):
        @pl.when((t >= lag) & (t < lag + CHUNKS))
        def _():
            fn(t - lag)

    def tick(t, _):
        stage(t, 0, choose)
        stage(t, 1, across)
        stage(t, 2, share)
        stage(t, 3, predict)
        stage(t, 4, gather)
        stage(t, 5, reduce_edge)
        stage(t, 6, clean)

        @pl.when(t == 0)
        def _():
            filters_one()
            spectra_one()
            ranks()

        @pl.when(t == 1)
        def _():
            filters_two()
            spectra_two()

        @pl.when(t == 2)
        def _():
            filters_three()

        @pl.when(t + AHEAD < CHUNKS)
        def _():
            start_first(t + AHEAD, 0)

        stage(t, 3, prepare)
        return 0

    lax.fori_loop(0, CHUNKS + 6, tick, 0)

    top, rest = split(cleaned[...].reshape(ROWS, QUARTER))
    clean_hi[...] = top
    clean_lo[...] = rest

    me = shot_of(x, z, h, c)
    group = 128 // SUB

    def deal(t):
        return remote(packed.at[t], arrive.at[me], ds, dr, (t, f))

    def place_rows(i, _):
        g = lax.rem(me // group + i, SHARDS // group)
        ids = lax.broadcasted_iota(I32, (128, ROWS), 0) + g * 128
        pick = jnp.where(ids == slots[...], 1.0, 0.0).astype(B16)
        block = dot(pick, clean_hi[...]) + dot(pick, clean_lo[...])
        packed[pl.ds(g * group, group)] = block.reshape(group, SUB, QUARTER)

        def send(j, _):
            t = g * group + lax.rem(me + j, group)

            @pl.when(t != me)
            def _():
                deal(t).start()

            return 0

        lax.fori_loop(0, group, send, 0)
        return 0

    lax.fori_loop(0, SHARDS // group, place_rows, 0)
    arrive[me] = packed[me]

    def finish(k, _):
        each(PIECES, lambda j: first(k, j, to_p).wait_send())
        each(NZ, lambda j: second(k, j, to_z).wait_send())
        third(k).wait_send()
        each(NZ, lambda j: fourth(k, j, to_z).wait_send())
        each(PIECES, lambda j: fifth(k, j, to_p).wait_send())
        sixth(k, f).wait_send()

        @pl.when(~inner)
        def _():
            farther(k).wait_send()

        @pl.when(inner)
        def _():
            partial_sum(k).wait_send()

        return 0

    lax.fori_loop(0, CHUNKS, finish, 0)
    each(NQ, lambda j: spec_f(j, to_f).wait_send())
    each(PIECES, lambda j: spec_p(j, to_p).wait_send())
    each(PIECES, lambda j: filt_p(j, to_p).wait_send())
    each(NZ, lambda j: filt_z(j, to_z).wait_send())
    filt_h(h).wait_send()
    others = pl.ds(0, SHARDS - 1)
    pltpu.make_async_copy(packed.at[others], packed.at[others], ds).wait()
    pltpu.make_async_copy(arrive.at[others], arrive.at[others], dr).wait()
    pairs_of = lax.broadcasted_iota(I32, (SUB, QUARTER), 0) // MOST

    def sort_rows(i, _):
        for b in range(SUB // MOST):
            total = arrive[4 * i]
            if b:
                total = pltpu.roll(total, SUB - MOST * b, 0)
            for j in range(1, 4):
                turn = MOST * (j - b) % SUB
                other = arrive[4 * i + j]
                if turn:
                    other = pltpu.roll(other, turn, 0)
                total = jnp.where(pairs_of == j, other, total)
            sorted_rows[b, pl.ds(pl.multiple_of(i * SUB, SUB), SUB), :] = total
        return 0

    lax.fori_loop(0, SHARDS // 4, sort_rows, 0)


def spread(*args):
    dma = pltpu.SemaphoreType.DMA
    v = pltpu.VMEM
    tile = (SUB, LANES)
    vm = pl.BlockSpec(memory_space=pltpu.VMEM)
    sm = pl.BlockSpec(memory_space=pltpu.SMEM)
    hbm = pl.BlockSpec(memory_space=pltpu.HBM)
    small = (STEPS, PAIR, *tile)
    wide = (NQ + 1) * LANES
    return pl.pallas_call(
        spread_kernel,
        out_shape=jax.ShapeDtypeStruct((SUB // MOST, SHARDS * MOST, QUARTER), F32),
        in_specs=[hbm, hbm, hbm, sm, sm] + [hbm] * 9,
        out_specs=vm,
        scratch_shapes=[
            v((SHARDS, SUB, QUARTER), F32), v((SHARDS, SUB, QUARTER), F32),
            v((SHOTS, PIECES, CHUNKS, SUB, QUARTER), F32),
            v((SHOTS, R), I32), v((SHOTS, 1, R), I32), v((4, TAPS), F32),
            v((128, 2 * wide), B16), v((128, 2 * wide), B16),
            v((NQ, SHOTS, PIECES, CHUNKS, *tile), F32),
            v((NH, NZ, PIECES, 128), F32),
            v((QUARTER, NQ * LANES), F32),
            v((NQ * LANES, 128), B16), v((NQ * LANES, 128), B16),
            v((wide, QUARTER), B16), v((wide, QUARTER), B16),
            v((NQ * LANES, 128), B16), v((NQ * LANES, 128), B16),
            v((wide, QUARTER), B16), v((wide, QUARTER), B16),
            v((CHUNKS, SHOTS * PIECES * SUB, QUARTER), F32),
            v((CHUNKS, SHOTS * PIECES * SUB, QUARTER), F32),
            v((COLS, R), F32),
            v((CHUNKS, 2 * (NQ + 1), SHOTS * PIECES * SUB, LANES), F32),
            v((SHOTS, PIECES, CHUNKS, SUB, QUARTER), F32),
            v((ROWS, QUARTER), B16), v((ROWS, QUARTER), B16),
            v((1, ROWS), I32),
            v((SUB, R), I32),
            v((SHOTS, PIECES, CHUNKS, SUB, 1), I32),
            v((SHOTS, PIECES, CHUNKS, SUB, 1), I32),
            v((SUB, 128), F32),
            v((4, PIECES, 128), F32),
            v((CHUNKS, PIECES, POINTS_BLK, *tile), F32),
            v((CHUNKS, STEPS, POINTS_BLK, *tile), F32),
            v((CHUNKS, NZ, *small), F32),
            v((CHUNKS, *small), F32),
            v((CHUNKS, *small), F32),
            v((CHUNKS, NZ, *small), F32),
            v((NQ, SHOTS * COLS, LANES), F32),
            v((NQ, SHOTS * COLS, LANES), F32),
            v((PIECES, SHOTS * COLS, LANES), F32),
            v((PIECES, SHOTS * COLS, LANES), F32),
            v((PIECES, SHOTS * COLS, LANES), F32),
            v((NZ, *small), F32),
            v((PIECES, SHOTS, CHUNKS, *tile), F32),
            v((PIECES, 8, 128), F32),
            v((PIECES, 128), F32),
            dma((CHUNKS, PIECES)), dma((CHUNKS, PIECES)),
            dma((CHUNKS, NZ)), dma((CHUNKS, NZ)),
            dma((CHUNKS,)), dma((CHUNKS,)),
            dma((CHUNKS, NZ)), dma((CHUNKS, NZ)),
            dma((CHUNKS, PIECES)), dma((CHUNKS, PIECES)),
            dma((CHUNKS, 2)), dma((CHUNKS, NQ)),
            dma((CHUNKS,)), dma((CHUNKS,)),
            dma((NQ,)), dma((NQ,)),
            dma((PIECES,)), dma((PIECES,)),
            dma((PIECES,)), dma((PIECES,)),
            dma((NZ,)), dma((NZ,)),
            dma, dma,
            dma((CHUNKS,)),
            dma((15,)),
            dma, dma,
        ],
        compiler_params=pltpu.CompilerParams(
            collective_id=0, has_side_effects=True, vmem_limit_bytes=60 * 2**20
        ),
    )(*args)


def on_device(traces, live_mask, offset_bin, surface, block_owner, point_column, filters):
    return spread(
        traces.reshape(SHOTS, PIECES, CHUNKS, SUB, QUARTER),
        live_mask,
        offset_bin.reshape(SHOTS, 1, R),
        point_column,
        block_owner,
        surface,
        filters,
        *(jnp.asarray(a) for a in (FORWARD, EDGE_HI, EDGE_LO, COMBINE_HI, COMBINE_LO)),
        jnp.asarray(TAP_HI),
        jnp.asarray(TAP_LO),
    )


def solution(mesh):
    return jax.shard_map(
        on_device,
        mesh=mesh,
        in_specs=(
            P("shot", None, "freq"),
            P("shot", None),
            P("shot", None, None),
            P("shot", None, "freq"),
            P(),
            P(),
            P("shot", None),
        ),
        out_specs=P("shot", None, "freq"),
        check_vma=False,
    )
```

```python
import jax
import jax.numpy as jnp
import ml_dtypes
import numpy as np
from jax import lax
from jax.experimental import pallas as pl
from jax.experimental.pallas import tpu as pltpu
from jax.sharding import PartitionSpec as P

NT = 1024
NF = 256
TAPS = 31
POINTS_BLK = 16
STEPS = 2
NX, NZ, NH, NC = 4, 8, 2, 2
NQ = 4
BAND = NF // NQ
LANES = 2 * BAND
QUARTER = NT // NQ
R = 256
SHOTS = 3
MOST = 2
SHARDS = NX * NZ * NH * NC
ROWS = SHOTS * R
PIECES = NX * NC
CHUNKS = 4
AHEAD = 2
SUB = 8
COLS = STEPS * POINTS_BLK
PAIR = POINTS_BLK // NZ
EDGE = (TAPS - 1) // 2
FULL = lax.Precision.HIGHEST
MESH = pl.DeviceIdType.MESH
F32 = jnp.float32
B16 = jnp.bfloat16
I32 = jnp.int32


def tables():
    t = np.arange(NT)
    m = np.arange(NF) + 1
    phase = 2 * np.pi * ((m[:, None] * t[None, :]) % NT) / NT
    real = np.cos(phase).reshape(NQ, BAND, NT)
    imag = -np.sin(phase).reshape(NQ, BAND, NT)
    wave = np.concatenate([real, imag], axis=1).reshape(NQ * LANES, NT)
    forward = wave.T.reshape(NQ, QUARTER, NQ * LANES)
    synth = wave * (2.0 / NT)
    k = np.arange(64)
    u = np.arange(EDGE)
    turn = 2 * np.pi * ((u[:, None] * k[None, :]) % 64) / 64
    short = np.concatenate([np.cos(turn), -np.sin(turn)], axis=1)
    edge = np.zeros((NQ, NQ * LANES, 128))
    edge[0] = synth[:, NT - EDGE :] @ short
    edge[NQ - 1] = synth[:, :EDGE] @ short
    back = np.zeros((NQ, 128, QUARTER))

    def inverse(n):
        a = 2 * np.pi * ((k[:, None] * n[None, :]) % 64) / 64
        return -np.concatenate([np.cos(a), -np.sin(a)], axis=0) / 64

    back[0][:, :EDGE] = inverse(np.arange(2 * EDGE, 3 * EDGE))
    back[NQ - 1][:, QUARTER - EDGE :] = inverse(np.arange(EDGE))
    combine = np.concatenate(
        [synth.reshape(NQ * LANES, NQ, QUARTER).transpose(1, 0, 2), back], axis=1
    )
    i = np.arange(TAPS)
    lag = 2 * np.pi * (((i[:, None] - EDGE) * m[None, :]) % NT) / NT
    c, s = np.cos(lag).reshape(TAPS, NQ, BAND), np.sin(lag).reshape(TAPS, NQ, BAND)
    same = np.concatenate([c, c], axis=2).reshape(TAPS, NQ * LANES)
    cross = np.concatenate([s, -s], axis=2).reshape(TAPS, NQ * LANES)
    lag2 = 2 * np.pi * ((i[:, None] * k[None, :]) % 64) / 64
    same2 = np.concatenate([np.cos(lag2), np.cos(lag2)], axis=1)
    cross2 = np.concatenate([np.sin(lag2), -np.sin(lag2)], axis=1)
    taps = np.concatenate([same, same2, cross, cross2], axis=1)
    taps = np.concatenate([taps] * 4 + [np.zeros((4, taps.shape[1]))], axis=0)
    return forward, edge, combine, taps


def halves(a):
    top = a.astype(ml_dtypes.bfloat16)
    return top, (a - top.astype(np.float64)).astype(ml_dtypes.bfloat16)


FORWARD, EDGE_IN, COMBINE, TAP_TABLE = tables()
FORWARD = FORWARD.astype(np.float32)
EDGE_HI, EDGE_LO = halves(EDGE_IN)
COMBINE_HI, COMBINE_LO = halves(COMBINE)
TAP_HI, TAP_LO = halves(TAP_TABLE)


def dot(a, b):
    return jnp.dot(a, b, preferred_element_type=F32)


def split(a):
    top = a.astype(B16)
    return top, (a - top.astype(F32)).astype(B16)


def dot3(a, top, low):
    a_top, a_low = split(a)
    return dot(a_top, top) + (dot(a_low, top) + dot(a_top, low))


def place():
    d = lax.axis_index("shot")
    x, z = d // (NZ * NH * NC), d // (NH * NC) % NZ
    return x, z, d // NC % NH, d % NC, lax.axis_index("freq")


def shot_of(x, z, h, c):
    return ((x * NZ + z) * NH + h) * NC + c


def spread_kernel(
    traces_in, live_in, bins_in, cols, owner, surface, filters_in,
    wave_all, edge_hi_all, edge_lo_all, combine_hi_all, combine_lo_all, tap_hi_in, tap_lo_in,
    sorted_rows,
    arrive, packed, traces, live, bins, filters, tap_hi, tap_lo,
    bands, table, wave, edge_hi, edge_lo, combine_hi, combine_lo,
    out_edge_hi, out_edge_lo, out_combine_hi, out_combine_lo, part_out, part_in,
    onehot, factor, cleaned, clean_hi, clean_lo, slots, rows8, bin_col, live_col, filt, f1x,
    r1, m, r2, hown, hin, ag, specp, specr, specall, sa, sb, srot, pred, f1, f1c,
    s1s, s1r, s2s, s2r, hs, hr, gs, gr, bs, br, fs, fr, qs, qr,
    ps, pr, cs, cr, u1s, u1r, u2s, u2r, us, ur, own, consts, ds, dr,
):
    x, z, h, c, f = place()
    mine = x * NC + c

    def dev_p(j):
        p = lax.rem(mine + j, PIECES)
        return p, (shot_of(p // NC, z, h, lax.rem(p, NC)), f)

    def dev_z(j):
        o = lax.rem(z + j, NZ)
        return o, (shot_of(x, o, h, c), f)

    def dev_f(j):
        o = lax.rem(f + j, NQ)
        return o, (shot_of(x, z, h, c), o)

    other_h = (shot_of(x, z, 1 - h, c), f)

    inner = (f == 1) | (f == 2)
    outer = jnp.where(f < 2, 0, NQ - 1)
    inside = jnp.where(f < 2, 1, 2)
    pairs = (
        (filters_in, filters), (live_in, live), (bins_in, bins), (traces_in, traces),
        (wave_all.at[f], wave), (tap_hi_in, tap_hi), (tap_lo_in, tap_lo),
        (edge_hi_all.at[f], edge_hi), (edge_lo_all.at[f], edge_lo),
        (combine_hi_all.at[f], combine_hi), (combine_lo_all.at[f], combine_lo),
        (edge_hi_all.at[outer], out_edge_hi), (edge_lo_all.at[outer], out_edge_lo),
        (combine_hi_all.at[outer], out_combine_hi), (combine_lo_all.at[outer], out_combine_lo),
    )
    held = [pltpu.make_async_copy(a, b, consts.at[i]) for i, (a, b) in enumerate(pairs)]
    for one in held:
        one.start()

    barrier = pltpu.get_barrier_semaphore()

    def greet(dev):
        pl.semaphore_signal(barrier, inc=1, device_id=dev, device_id_type=MESH)

    def each(count, fn):
        def body(j, _):
            fn(j)
            return 0

        lax.fori_loop(1, count, body, 0)

    each(PIECES, lambda j: greet(dev_p(j)[1]))
    each(NZ, lambda j: greet(dev_z(j)[1]))
    each(NQ, lambda j: greet(dev_f(j)[1]))
    greet(other_h)
    pl.semaphore_wait(barrier, PIECES - 1 + NZ - 1 + NQ - 1 + 1)

    def remote(src, dst, send, recv, dev):
        return pltpu.make_async_remote_copy(
            src_ref=src, dst_ref=dst, send_sem=send, recv_sem=recv,
            device_id=dev, device_id_type=MESH,
        )

    def first(k, j, at):
        p, dev = dev_p(j)
        src = surface.at[:, pl.ds(pl.multiple_of(p * (CHUNKS * SUB) + k * SUB, SUB), SUB), :]
        return remote(src, r1.at[k, at(p)], s1s.at[k, p], s1r.at[k, at(p)], dev)

    def second(k, j, at):
        o, dev = dev_z(j)
        return remote(
            m.at[k, :, pl.ds(o * PAIR, PAIR)], r2.at[k, at(o)], s2s.at[k, o], s2r.at[k, at(o)], dev
        )

    def third(k):
        return remote(hown.at[k], hin.at[k], hs.at[k], hr.at[k], other_h)

    def fourth(k, j, at):
        o, dev = dev_z(j)
        return remote(ag.at[k, z], ag.at[k, at(o)], gs.at[k, o], gr.at[k, at(o)], dev)

    def fifth(k, j, at):
        p, dev = dev_p(j)
        return remote(
            pred.at[p, :, k], bands.at[f, :, at(p), k], bs.at[k, p], br.at[k, at(p)], dev
        )

    beside = (shot_of(x, z, h, c), jnp.where(inner, NQ - 1 - f, inside))
    beyond = (shot_of(x, z, h, c), NQ - 1 - inside)
    edge_dev = (shot_of(x, z, h, c), outer)

    def sixth(k, o):
        return remote(bands.at[f, :, :, k], bands.at[o, :, :, k], fs.at[k, 0], fr.at[k, o], beside)

    def farther(k):
        return remote(
            bands.at[f, :, :, k], bands.at[f, :, :, k], fs.at[k, 1], fr.at[k, f], beyond
        )

    def partial_sum(k):
        return remote(part_out.at[k], part_in.at[k], qs.at[k], qr.at[k], edge_dev)

    def spec_f(j, at):
        o, dev = dev_f(j)
        return remote(specp.at[o], specr.at[at(o)], ps.at[o], pr.at[at(o)], dev)

    def spec_p(j, at):
        p, dev = dev_p(j)
        return remote(specall.at[mine], specall.at[at(p)], cs.at[p], cr.at[at(p)], dev)

    def filt_p(j, at):
        p, dev = dev_p(j)
        return remote(filt, f1.at[at(p)], u1s.at[p], u1r.at[at(p)], dev)

    def filt_z(j, at):
        o, dev = dev_z(j)
        return remote(f1c, table.at[h, at(o)], u2s.at[o], u2r.at[at(o)], dev)

    def filt_h(at):
        return remote(table.at[h], table.at[at], us, ur, other_h)

    def to_p(p):
        return mine

    def to_z(o):
        return z

    def to_f(o):
        return f

    def here(o):
        return o

    def start_first(k, _):
        each(PIECES, lambda j: first(k, j, to_p).start())
        return 0

    start_first(0, 0)
    filt[...] = jnp.zeros((SUB, 128), F32)
    held[0].wait()
    filt[0:4, 0:TAPS] = filters[...]
    each(PIECES, lambda j: filt_p(j, to_p).start())

    lax.fori_loop(1, AHEAD, start_first, 0)

    def own_piece(k):
        src = surface.at[:, pl.ds(pl.multiple_of(mine * (CHUNKS * SUB) + k * SUB, SUB), SUB), :]
        return pltpu.make_async_copy(src, r1.at[k, mine], own.at[k])

    for k in range(CHUNKS):
        own_piece(k).start()

    weights = []
    for b in range(STEPS):
        who = owner[b]
        who_p = (who >> 5) * NC + (who & 1)
        who_z = (who >> 2) & (NZ - 1)
        who_h = (who >> 1) & 1
        weights.append(
            [jnp.where(who_p == p, 1.0, 0.0) for p in range(PIECES)]
            + [jnp.where(who_z == o, 1.0, 0.0) for o in range(NZ)]
            + [jnp.where(who_h == h, 1.0, 0.0), jnp.where(who_h == h, 0.0, 1.0)]
        )

    lane_row = lax.broadcasted_iota(I32, (1, R), 1)
    for b in range(STEPS):
        for j in range(POINTS_BLK):
            row = b * POINTS_BLK + j
            onehot[row : row + 1, :] = jnp.where(lane_row == cols[b, j], 1.0, 0.0)
    for one in held[1:5]:
        one.wait()
    picked = []
    for s in range(SHOTS):
        pick = onehot[...] * live[s : s + 1, :].astype(F32)
        picked.append(
            jnp.dot(
                pick, traces[s].reshape(R, QUARTER), precision=FULL, preferred_element_type=F32
            )
        )
    part = jnp.dot(
        jnp.concatenate(picked, axis=0), wave[...], precision=FULL, preferred_element_type=F32
    )
    for o in range(NQ):
        specp[o] = part[:, o * LANES : (o + 1) * LANES]
    each(NQ, lambda j: spec_f(j, to_f).start())
    specr[f] = specp[f]
    f1[mine] = filt[...]

    def filters_one():
        each(PIECES, lambda j: filt_p(j, here).wait_recv())
        for p in range(PIECES):
            for i in range(4):
                f1x[i, p : p + 1, :] = f1[p, i : i + 1, :]
        lined = f1x[0]
        for i in range(1, 4):
            lined = lined + pltpu.roll(f1x[i], i * TAPS, 1)
        f1c[...] = lined
        each(NZ, lambda j: filt_z(j, to_z).start())
        table[h, z] = f1c[...]

    def filters_two():
        each(NZ, lambda j: filt_z(j, here).wait_recv())
        filt_h(h).start()

    def filters_three():
        filt_h(1 - h).wait_recv()
        for one in held[5:]:
            one.wait()

    def spectra_one():
        each(NQ, lambda j: spec_f(j, here).wait_recv())
        specall[mine] = specr[0] + specr[1] + specr[2] + specr[3]
        each(PIECES, lambda j: spec_p(j, to_p).start())

    def spectra_two():
        each(PIECES, lambda j: spec_p(j, here).wait_recv())
        low = lax.broadcasted_iota(I32, (SHOTS * COLS, LANES), 1) < BAND

        def both(p, _):
            v = specall[p]
            w = pltpu.roll(v, BAND, 1)
            sa[p] = jnp.where(low, v, w)
            sb[p] = jnp.where(low, -w, v)
            return 0

        lax.fori_loop(0, PIECES, both, 0)

    def ranks():
        rows8[...] = jnp.zeros((SUB, R), I32)
        rows8[0:SHOTS, :] = bins[...].reshape(SHOTS, R)
        rows8[SHOTS : 2 * SHOTS, :] = live[...]
        turned_rows = rows8[...].T
        for s in range(SHOTS):
            bin_col[s] = turned_rows[:, s : s + 1].reshape(PIECES, CHUNKS, SUB, 1)
            live_col[s] = turned_rows[:, SHOTS + s : SHOTS + s + 1].reshape(
                PIECES, CHUNKS, SUB, 1
            )
        for s in range(SHOTS):
            row = bins[s]
            count = jnp.zeros((1, R), I32)
            for o in range(s + 1):
                hit = jnp.where(turned_rows[:, o : o + 1] == row, 1, 0)
                if o == s:
                    before = lax.broadcasted_iota(I32, (R, R), 0) < lax.broadcasted_iota(
                        I32, (R, R), 1
                    )
                    hit = jnp.where(before, hit, 0)
                count = count + jnp.sum(hit, axis=0, keepdims=True)
            slots[:, s * R : (s + 1) * R] = row * 2 + count

    def predict(k):
        each(NZ, lambda j: fourth(k, j, here).wait_recv())
        srot[...] = pltpu.roll(
            ag[k].reshape(NZ * STEPS * PAIR * SUB, LANES), BAND, 1
        ).reshape(NZ, STEPS, PAIR, SUB, LANES)

        def piece(p, _):
            totals = [jnp.zeros((SUB, LANES), F32) for _ in range(SHOTS)]
            for o in range(NZ):
                for b in range(STEPS):
                    for i in range(PAIR):
                        straight, turned = ag[k, o, b, i], srot[o, b, i]
                        for s in range(SHOTS):
                            row = s * COLS + b * POINTS_BLK + o * PAIR + i
                            totals[s] = (
                                totals[s]
                                + sa[p, row : row + 1, :] * straight
                                + sb[p, row : row + 1, :] * turned
                            )
            for s in range(SHOTS):
                pred[p, s, k] = totals[s]
            return 0

        lax.fori_loop(0, PIECES, piece, 0)
        each(PIECES, lambda j: fifth(k, j, to_p).start())
        for s in range(SHOTS):
            bands[f, s, mine, k] = pred[mine, s, k]

    def choose(k):
        own_piece(k).wait()
        each(PIECES, lambda j: first(k, j, here).wait_recv())
        for b in range(STEPS):
            total = jnp.zeros((POINTS_BLK, SUB, LANES), F32)
            for p in range(PIECES):
                total = total + weights[b][p] * r1[k, p]
            m[k, b] = total
        each(NZ, lambda j: second(k, j, to_z).start())
        for b in range(STEPS):
            r2[k, z, b] = m[k, b, pl.ds(z * PAIR, PAIR)]

    def gather(k):
        each(PIECES, lambda j: fifth(k, j, here).wait_recv())
        @pl.when(~inner)
        def _():
            farther(k).start()

        sixth(k, f).start()

    def across(k):
        each(NZ, lambda j: second(k, j, here).wait_recv())
        for b in range(STEPS):
            total = jnp.zeros((PAIR, SUB, LANES), F32)
            for o in range(NZ):
                total = total + weights[b][PIECES + o] * r2[k, o, b]
            hown[k, b] = total
        third(k).start()

    def share(k):
        third(k).wait_recv()
        for b in range(STEPS):
            ag[k, z, b] = (
                weights[b][PIECES + NZ] * hown[k, b] + weights[b][PIECES + NZ + 1] * hin[k, b]
            )
        each(NZ, lambda j: fourth(k, j, to_z).start())

    tile = SHOTS * PIECES * SUB

    def prepare(k):
        lane = lax.broadcasted_iota(I32, (tile, 128), 1)
        one = bin_col[:, :, k].reshape(tile, 1)
        home = one >> 2
        line = ((home >> 1) & 1) * (NZ * PIECES) + ((home >> 2) & (NZ - 1)) * PIECES
        line = line + (home >> 5) * NC + (home & 1)
        pick = jnp.where(lane == line, 1.0, 0.0).astype(B16)
        all_taps = table[...].reshape(128, 128)
        top, rest = split(all_taps)
        middle, last = split(all_taps - top.astype(F32))
        four = dot(pick, top) + (dot(pick, middle) + dot(pick, last))
        start = (one & 3) * TAPS
        four = jnp.where((lane >= start) & (lane < start + TAPS), four, 0.0)
        answer = dot3(four, tap_hi[...], tap_lo[...])
        for o in range(2 * (NQ + 1)):
            factor[k, o] = answer[:, o * LANES : (o + 1) * LANES]

    def filtered(k, order, e_hi, e_lo, c_hi, c_lo):
        ends = jnp.zeros((tile, 128), F32)
        total = jnp.zeros((tile, QUARTER), F32)

        def mix(block, o, span):
            mixed = block * factor[k, o] + pltpu.roll(block, BAND, 1) * factor[k, NQ + 1 + o]
            return dot3(mixed, c_hi[span, :], c_lo[span, :])

        for o in order:
            span = pl.ds(pl.multiple_of(o * LANES, LANES), LANES)
            block = bands[o, :, :, k].reshape(tile, LANES)
            ends = ends + dot3(block, e_hi[span, :], e_lo[span, :])
            total = total + mix(block, o, span)
        return total + mix(ends, NQ, slice(NQ * LANES, (NQ + 1) * LANES))

    def reduce_edge(k):
        @pl.when(inner)
        def _():
            sixth(k, outer).wait_recv()
            sixth(k, NQ - 1 - f).wait_recv()
            sixth(k, NQ - 1 - outer).wait_recv()
            part_out[k] = filtered(
                k, (f, NQ - 1 - f, NQ - 1 - outer),
                out_edge_hi, out_edge_lo, out_combine_hi, out_combine_lo,
            )
            partial_sum(k).start()

    def clean(k):
        def put(total):
            alive = live_col[:, :, k].reshape(tile, 1).astype(F32)
            whole = traces[:, :, k].reshape(tile, QUARTER)
            cleaned[:, :, k] = (alive * (whole - total)).reshape(SHOTS, PIECES, SUB, QUARTER)

        @pl.when(inner)
        def _():
            put(filtered(k, range(NQ), edge_hi, edge_lo, combine_hi, combine_lo))

        @pl.when(~inner)
        def _():
            mine_part = filtered(k, (f,), edge_hi, edge_lo, combine_hi, combine_lo)
            partial_sum(k).wait_recv()
            put(mine_part + part_in[k])

    def stage(t, lag, fn):
        @pl.when((t >= lag) & (t < lag + CHUNKS))
        def _():
            fn(t - lag)

    def tick(t, _):
        stage(t, 0, choose)
        stage(t, 1, across)
        stage(t, 2, share)
        stage(t, 3, predict)
        stage(t, 4, gather)
        stage(t, 5, reduce_edge)
        stage(t, 6, clean)

        @pl.when(t == 0)
        def _():
            filters_one()
            spectra_one()
            ranks()

        @pl.when(t == 1)
        def _():
            filters_two()
            spectra_two()

        @pl.when(t == 2)
        def _():
            filters_three()

        @pl.when(t + AHEAD < CHUNKS)
        def _():
            start_first(t + AHEAD, 0)

        stage(t, 3, prepare)
        return 0

    lax.fori_loop(0, CHUNKS + 6, tick, 0)

    top, rest = split(cleaned[...].reshape(ROWS, QUARTER))
    clean_hi[...] = top
    clean_lo[...] = rest

    me = shot_of(x, z, h, c)
    group = 128 // SUB

    def deal(t):
        return remote(packed.at[t], arrive.at[me], ds, dr.at[me // group], (t, f))

    def place_rows(i, _):
        g = lax.rem(me // group + i, SHARDS // group)
        ids = lax.broadcasted_iota(I32, (128, ROWS), 0) + g * 128
        pick = jnp.where(ids == slots[...], 1.0, 0.0).astype(B16)
        block = dot(pick, clean_hi[...]) + dot(pick, clean_lo[...])
        packed[pl.ds(g * group, group)] = block.reshape(group, SUB, QUARTER)

        def send(j, _):
            t = g * group + lax.rem(me + j, group)

            @pl.when(t != me)
            def _():
                deal(t).start()

            return 0

        lax.fori_loop(0, group, send, 0)
        return 0

    lax.fori_loop(0, SHARDS // group, place_rows, 0)
    arrive[me] = packed[me]

    def finish(k, _):
        each(PIECES, lambda j: first(k, j, to_p).wait_send())
        each(NZ, lambda j: second(k, j, to_z).wait_send())
        third(k).wait_send()
        each(NZ, lambda j: fourth(k, j, to_z).wait_send())
        each(PIECES, lambda j: fifth(k, j, to_p).wait_send())
        sixth(k, f).wait_send()

        @pl.when(~inner)
        def _():
            farther(k).wait_send()

        @pl.when(inner)
        def _():
            partial_sum(k).wait_send()

        return 0

    lax.fori_loop(0, CHUNKS, finish, 0)
    each(NQ, lambda j: spec_f(j, to_f).wait_send())
    each(PIECES, lambda j: spec_p(j, to_p).wait_send())
    each(PIECES, lambda j: filt_p(j, to_p).wait_send())
    each(NZ, lambda j: filt_z(j, to_z).wait_send())
    filt_h(h).wait_send()
    pairs_of = lax.broadcasted_iota(I32, (SUB, QUARTER), 0) // MOST

    def came(g, count):
        some = arrive.at[pl.ds(0, count)]
        pltpu.make_async_copy(some, some, dr.at[g]).wait()

    def sort_group(n, _):
        g = lax.rem(me // group + SHARDS // group - n, SHARDS // group)

        @pl.when(n == 0)
        def _():
            came(g, group - 1)

        @pl.when(n != 0)
        def _():
            came(g, group)

        def sort_rows(s, _):
            i = g * (group // 4) + s
            for b in range(SUB // MOST):
                total = arrive[4 * i]
                if b:
                    total = pltpu.roll(total, SUB - MOST * b, 0)
                for j in range(1, 4):
                    turn = MOST * (j - b) % SUB
                    other = arrive[4 * i + j]
                    if turn:
                        other = pltpu.roll(other, turn, 0)
                    total = jnp.where(pairs_of == j, other, total)
                sorted_rows[b, pl.ds(pl.multiple_of(i * SUB, SUB), SUB), :] = total
            return 0

        lax.fori_loop(0, group // 4, sort_rows, 0)
        return 0

    lax.fori_loop(0, SHARDS // group, sort_group, 0)
    others = packed.at[pl.ds(0, SHARDS - 1)]
    pltpu.make_async_copy(others, others, ds).wait()


def spread(*args):
    dma = pltpu.SemaphoreType.DMA
    v = pltpu.VMEM
    tile = (SUB, LANES)
    vm = pl.BlockSpec(memory_space=pltpu.VMEM)
    sm = pl.BlockSpec(memory_space=pltpu.SMEM)
    hbm = pl.BlockSpec(memory_space=pltpu.HBM)
    small = (STEPS, PAIR, *tile)
    wide = (NQ + 1) * LANES
    return pl.pallas_call(
        spread_kernel,
        out_shape=jax.ShapeDtypeStruct((SUB // MOST, SHARDS * MOST, QUARTER), F32),
        in_specs=[hbm, hbm, hbm, sm, sm] + [hbm] * 9,
        out_specs=vm,
        scratch_shapes=[
            v((SHARDS, SUB, QUARTER), F32), v((SHARDS, SUB, QUARTER), F32),
            v((SHOTS, PIECES, CHUNKS, SUB, QUARTER), F32),
            v((SHOTS, R), I32), v((SHOTS, 1, R), I32), v((4, TAPS), F32),
            v((128, 2 * wide), B16), v((128, 2 * wide), B16),
            v((NQ, SHOTS, PIECES, CHUNKS, *tile), F32),
            v((NH, NZ, PIECES, 128), F32),
            v((QUARTER, NQ * LANES), F32),
            v((NQ * LANES, 128), B16), v((NQ * LANES, 128), B16),
            v((wide, QUARTER), B16), v((wide, QUARTER), B16),
            v((NQ * LANES, 128), B16), v((NQ * LANES, 128), B16),
            v((wide, QUARTER), B16), v((wide, QUARTER), B16),
            v((CHUNKS, SHOTS * PIECES * SUB, QUARTER), F32),
            v((CHUNKS, SHOTS * PIECES * SUB, QUARTER), F32),
            v((COLS, R), F32),
            v((CHUNKS, 2 * (NQ + 1), SHOTS * PIECES * SUB, LANES), F32),
            v((SHOTS, PIECES, CHUNKS, SUB, QUARTER), F32),
            v((ROWS, QUARTER), B16), v((ROWS, QUARTER), B16),
            v((1, ROWS), I32),
            v((SUB, R), I32),
            v((SHOTS, PIECES, CHUNKS, SUB, 1), I32),
            v((SHOTS, PIECES, CHUNKS, SUB, 1), I32),
            v((SUB, 128), F32),
            v((4, PIECES, 128), F32),
            v((CHUNKS, PIECES, POINTS_BLK, *tile), F32),
            v((CHUNKS, STEPS, POINTS_BLK, *tile), F32),
            v((CHUNKS, NZ, *small), F32),
            v((CHUNKS, *small), F32),
            v((CHUNKS, *small), F32),
            v((CHUNKS, NZ, *small), F32),
            v((NQ, SHOTS * COLS, LANES), F32),
            v((NQ, SHOTS * COLS, LANES), F32),
            v((PIECES, SHOTS * COLS, LANES), F32),
            v((PIECES, SHOTS * COLS, LANES), F32),
            v((PIECES, SHOTS * COLS, LANES), F32),
            v((NZ, *small), F32),
            v((PIECES, SHOTS, CHUNKS, *tile), F32),
            v((PIECES, 8, 128), F32),
            v((PIECES, 128), F32),
            dma((CHUNKS, PIECES)), dma((CHUNKS, PIECES)),
            dma((CHUNKS, NZ)), dma((CHUNKS, NZ)),
            dma((CHUNKS,)), dma((CHUNKS,)),
            dma((CHUNKS, NZ)), dma((CHUNKS, NZ)),
            dma((CHUNKS, PIECES)), dma((CHUNKS, PIECES)),
            dma((CHUNKS, 2)), dma((CHUNKS, NQ)),
            dma((CHUNKS,)), dma((CHUNKS,)),
            dma((NQ,)), dma((NQ,)),
            dma((PIECES,)), dma((PIECES,)),
            dma((PIECES,)), dma((PIECES,)),
            dma((NZ,)), dma((NZ,)),
            dma, dma,
            dma((CHUNKS,)),
            dma((15,)),
            dma, dma((8,)),
        ],
        compiler_params=pltpu.CompilerParams(
            collective_id=0, has_side_effects=True, vmem_limit_bytes=60 * 2**20
        ),
    )(*args)


def on_device(traces, live_mask, offset_bin, surface, block_owner, point_column, filters):
    return spread(
        traces.reshape(SHOTS, PIECES, CHUNKS, SUB, QUARTER),
        live_mask,
        offset_bin.reshape(SHOTS, 1, R),
        point_column,
        block_owner,
        surface,
        filters,
        *(jnp.asarray(a) for a in (FORWARD, EDGE_HI, EDGE_LO, COMBINE_HI, COMBINE_LO)),
        jnp.asarray(TAP_HI),
        jnp.asarray(TAP_LO),
    )


def solution(mesh):
    return jax.shard_map(
        on_device,
        mesh=mesh,
        in_specs=(
            P("shot", None, "freq"),
            P("shot", None),
            P("shot", None, None),
            P("shot", None, "freq"),
            P(),
            P(),
            P("shot", None),
        ),
        out_specs=P("shot", None, "freq"),
        check_vma=False,
    )
```

```python
import jax
import jax.numpy as jnp
import ml_dtypes
import numpy as np
from jax import lax
from jax.experimental import pallas as pl
from jax.experimental.pallas import tpu as pltpu
from jax.sharding import PartitionSpec as P

NT = 1024
NF = 256
TAPS = 31
POINTS_BLK = 16
STEPS = 2
NX, NZ, NH, NC = 4, 8, 2, 2
NQ = 4
BAND = NF // NQ
LANES = 2 * BAND
QUARTER = NT // NQ
R = 256
SHOTS = 3
MOST = 2
SHARDS = NX * NZ * NH * NC
ROWS = SHOTS * R
PIECES = NX * NC
CHUNKS = 4
AHEAD = 2
SUB = 8
COLS = STEPS * POINTS_BLK
PAIR = POINTS_BLK // NZ
EDGE = (TAPS - 1) // 2
FULL = lax.Precision.HIGHEST
MESH = pl.DeviceIdType.MESH
F32 = jnp.float32
B16 = jnp.bfloat16
I32 = jnp.int32


def tables():
    t = np.arange(NT)
    m = np.arange(NF) + 1
    phase = 2 * np.pi * ((m[:, None] * t[None, :]) % NT) / NT
    real = np.cos(phase).reshape(NQ, BAND, NT)
    imag = -np.sin(phase).reshape(NQ, BAND, NT)
    wave = np.concatenate([real, imag], axis=1).reshape(NQ * LANES, NT)
    forward = wave.T.reshape(NQ, QUARTER, NQ * LANES)
    synth = wave * (2.0 / NT)
    k = np.arange(64)
    u = np.arange(EDGE)
    turn = 2 * np.pi * ((u[:, None] * k[None, :]) % 64) / 64
    short = np.concatenate([np.cos(turn), -np.sin(turn)], axis=1)
    edge = np.zeros((NQ, NQ * LANES, 128))
    edge[0] = synth[:, NT - EDGE :] @ short
    edge[NQ - 1] = synth[:, :EDGE] @ short
    back = np.zeros((NQ, 128, QUARTER))

    def inverse(n):
        a = 2 * np.pi * ((k[:, None] * n[None, :]) % 64) / 64
        return -np.concatenate([np.cos(a), -np.sin(a)], axis=0) / 64

    back[0][:, :EDGE] = inverse(np.arange(2 * EDGE, 3 * EDGE))
    back[NQ - 1][:, QUARTER - EDGE :] = inverse(np.arange(EDGE))
    combine = np.concatenate(
        [synth.reshape(NQ * LANES, NQ, QUARTER).transpose(1, 0, 2), back], axis=1
    )
    i = np.arange(TAPS)
    lag = 2 * np.pi * (((i[:, None] - EDGE) * m[None, :]) % NT) / NT
    c, s = np.cos(lag).reshape(TAPS, NQ, BAND), np.sin(lag).reshape(TAPS, NQ, BAND)
    same = np.concatenate([c, c], axis=2).reshape(TAPS, NQ * LANES)
    cross = np.concatenate([s, -s], axis=2).reshape(TAPS, NQ * LANES)
    lag2 = 2 * np.pi * ((i[:, None] * k[None, :]) % 64) / 64
    same2 = np.concatenate([np.cos(lag2), np.cos(lag2)], axis=1)
    cross2 = np.concatenate([np.sin(lag2), -np.sin(lag2)], axis=1)
    taps = np.concatenate([same, same2, cross, cross2], axis=1)
    taps = np.concatenate([taps] * 4 + [np.zeros((4, taps.shape[1]))], axis=0)
    return forward, edge, combine, taps


def halves(a):
    top = a.astype(ml_dtypes.bfloat16)
    return top, (a - top.astype(np.float64)).astype(ml_dtypes.bfloat16)


FORWARD, EDGE_IN, COMBINE, TAP_TABLE = tables()
FORWARD = FORWARD.astype(np.float32)
EDGE_HI, EDGE_LO = halves(EDGE_IN)
COMBINE_HI, COMBINE_LO = halves(COMBINE)
TAP_HI, TAP_LO = halves(TAP_TABLE)


def dot(a, b):
    return jnp.dot(a, b, preferred_element_type=F32)


def split(a):
    top = a.astype(B16)
    return top, (a - top.astype(F32)).astype(B16)


def dot3(a, top, low):
    a_top, a_low = split(a)
    return dot(a_top, top) + (dot(a_low, top) + dot(a_top, low))


def place():
    d = lax.axis_index("shot")
    x, z = d // (NZ * NH * NC), d // (NH * NC) % NZ
    return x, z, d // NC % NH, d % NC, lax.axis_index("freq")


def shot_of(x, z, h, c):
    return ((x * NZ + z) * NH + h) * NC + c


def spread_kernel(
    traces_in, live_in, bins_in, cols, owner, surface, filters_in,
    wave_all, edge_hi_all, edge_lo_all, combine_hi_all, combine_lo_all, tap_hi_in, tap_lo_in,
    sorted_rows,
    arrive, packed, traces, live, bins, filters, tap_hi, tap_lo,
    bands, table, wave, edge_hi, edge_lo, combine_hi, combine_lo,
    out_edge_hi, out_edge_lo, out_combine_hi, out_combine_lo, part_out, part_in,
    onehot, factor, cleaned, clean_hi, clean_lo, slots, rows8, bin_col, live_col, filt, f1x,
    r1, m, r2, hown, hin, ag, specp, specr, specall, sa, sb, srot, pred, f1, f1c,
    s1s, s1r, s2s, s2r, hs, hr, gs, gr, bs, br, fs, fr, qs, qr,
    ps, pr, cs, cr, u1s, u1r, u2s, u2r, us, ur, own, consts, ds, dr,
):
    x, z, h, c, f = place()
    mine = x * NC + c

    def dev_p(j):
        p = lax.rem(mine + j, PIECES)
        return p, (shot_of(p // NC, z, h, lax.rem(p, NC)), f)

    def dev_z(j):
        o = lax.rem(z + j, NZ)
        return o, (shot_of(x, o, h, c), f)

    def dev_f(j):
        o = lax.rem(f + j, NQ)
        return o, (shot_of(x, z, h, c), o)

    other_h = (shot_of(x, z, 1 - h, c), f)

    inner = (f == 1) | (f == 2)
    outer = jnp.where(f < 2, 0, NQ - 1)
    inside = jnp.where(f < 2, 1, 2)
    pairs = (
        (filters_in, filters), (live_in, live), (bins_in, bins), (traces_in, traces),
        (wave_all.at[f], wave), (tap_hi_in, tap_hi), (tap_lo_in, tap_lo),
        (edge_hi_all.at[f], edge_hi), (edge_lo_all.at[f], edge_lo),
        (combine_hi_all.at[f], combine_hi), (combine_lo_all.at[f], combine_lo),
        (edge_hi_all.at[outer], out_edge_hi), (edge_lo_all.at[outer], out_edge_lo),
        (combine_hi_all.at[outer], out_combine_hi), (combine_lo_all.at[outer], out_combine_lo),
    )
    held = [pltpu.make_async_copy(a, b, consts.at[i]) for i, (a, b) in enumerate(pairs)]
    for one in held:
        one.start()

    barrier = pltpu.get_barrier_semaphore()

    def greet(dev):
        pl.semaphore_signal(barrier, inc=1, device_id=dev, device_id_type=MESH)

    def each(count, fn):
        def body(j, _):
            fn(j)
            return 0

        lax.fori_loop(1, count, body, 0)

    each(PIECES, lambda j: greet(dev_p(j)[1]))
    each(NZ, lambda j: greet(dev_z(j)[1]))
    each(NQ, lambda j: greet(dev_f(j)[1]))
    greet(other_h)
    pl.semaphore_wait(barrier, PIECES - 1 + NZ - 1 + NQ - 1 + 1)

    def remote(src, dst, send, recv, dev):
        return pltpu.make_async_remote_copy(
            src_ref=src, dst_ref=dst, send_sem=send, recv_sem=recv,
            device_id=dev, device_id_type=MESH,
        )

    def first(k, j, at):
        p, dev = dev_p(j)
        src = surface.at[:, pl.ds(pl.multiple_of(p * (CHUNKS * SUB) + k * SUB, SUB), SUB), :]
        return remote(src, r1.at[k, at(p)], s1s.at[k, p], s1r.at[k, at(p)], dev)

    def second(k, j, at):
        o, dev = dev_z(j)
        return remote(
            m.at[k, :, pl.ds(o * PAIR, PAIR)], r2.at[k, at(o)], s2s.at[k, o], s2r.at[k, at(o)], dev
        )

    def third(k):
        return remote(hown.at[k], hin.at[k], hs.at[k], hr.at[k], other_h)

    def fourth(k, j, at):
        o, dev = dev_z(j)
        return remote(ag.at[k, z], ag.at[k, at(o)], gs.at[k, o], gr.at[k, at(o)], dev)

    def fifth(k, j, at):
        p, dev = dev_p(j)
        return remote(
            pred.at[p, :, k], bands.at[f, :, at(p), k], bs.at[k, p], br.at[k, at(p)], dev
        )

    beside = (shot_of(x, z, h, c), jnp.where(inner, NQ - 1 - f, inside))
    beyond = (shot_of(x, z, h, c), NQ - 1 - inside)
    edge_dev = (shot_of(x, z, h, c), outer)

    def sixth(k, o):
        return remote(bands.at[f, :, :, k], bands.at[o, :, :, k], fs.at[k, 0], fr.at[k, o], beside)

    def farther(k):
        return remote(
            bands.at[f, :, :, k], bands.at[f, :, :, k], fs.at[k, 1], fr.at[k, f], beyond
        )

    def partial_sum(k):
        return remote(part_out.at[k], part_in.at[k], qs.at[k], qr.at[k], edge_dev)

    def spec_f(j, at):
        o, dev = dev_f(j)
        return remote(specp.at[o], specr.at[at(o)], ps.at[o], pr.at[at(o)], dev)

    def spec_p(j, at):
        p, dev = dev_p(j)
        return remote(specall.at[mine], specall.at[at(p)], cs.at[p], cr.at[at(p)], dev)

    def filt_p(j, at):
        p, dev = dev_p(j)
        return remote(filt, f1.at[at(p)], u1s.at[p], u1r.at[at(p)], dev)

    def filt_z(j, at):
        o, dev = dev_z(j)
        return remote(f1c, table.at[h, at(o)], u2s.at[o], u2r.at[at(o)], dev)

    def filt_h(at):
        return remote(table.at[h], table.at[at], us, ur, other_h)

    def to_p(p):
        return mine

    def to_z(o):
        return z

    def to_f(o):
        return f

    def here(o):
        return o

    def start_first(k, _):
        each(PIECES, lambda j: first(k, j, to_p).start())
        return 0

    start_first(0, 0)
    filt[...] = jnp.zeros((SUB, 128), F32)
    held[0].wait()
    filt[0:4, 0:TAPS] = filters[...]
    each(PIECES, lambda j: filt_p(j, to_p).start())

    lax.fori_loop(1, AHEAD, start_first, 0)

    def own_piece(k):
        src = surface.at[:, pl.ds(pl.multiple_of(mine * (CHUNKS * SUB) + k * SUB, SUB), SUB), :]
        return pltpu.make_async_copy(src, r1.at[k, mine], own.at[k])

    for k in range(CHUNKS):
        own_piece(k).start()

    weights = []
    for b in range(STEPS):
        who = owner[b]
        who_p = (who >> 5) * NC + (who & 1)
        who_z = (who >> 2) & (NZ - 1)
        who_h = (who >> 1) & 1
        weights.append(
            [jnp.where(who_p == p, 1.0, 0.0) for p in range(PIECES)]
            + [jnp.where(who_z == o, 1.0, 0.0) for o in range(NZ)]
            + [jnp.where(who_h == h, 1.0, 0.0), jnp.where(who_h == h, 0.0, 1.0)]
        )

    lane_row = lax.broadcasted_iota(I32, (1, R), 1)
    for b in range(STEPS):
        for j in range(POINTS_BLK):
            row = b * POINTS_BLK + j
            onehot[row : row + 1, :] = jnp.where(lane_row == cols[b, j], 1.0, 0.0)
    for one in held[1:5]:
        one.wait()
    picked = []
    for s in range(SHOTS):
        pick = onehot[...] * live[s : s + 1, :].astype(F32)
        picked.append(
            jnp.dot(
                pick, traces[s].reshape(R, QUARTER), precision=FULL, preferred_element_type=F32
            )
        )
    part = jnp.dot(
        jnp.concatenate(picked, axis=0), wave[...], precision=FULL, preferred_element_type=F32
    )
    for o in range(NQ):
        specp[o] = part[:, o * LANES : (o + 1) * LANES]
    each(NQ, lambda j: spec_f(j, to_f).start())
    specr[f] = specp[f]
    f1[mine] = filt[...]

    def filters_one():
        each(PIECES, lambda j: filt_p(j, here).wait_recv())
        for p in range(PIECES):
            for i in range(4):
                f1x[i, p : p + 1, :] = f1[p, i : i + 1, :]
        lined = f1x[0]
        for i in range(1, 4):
            lined = lined + pltpu.roll(f1x[i], i * TAPS, 1)
        f1c[...] = lined
        each(NZ, lambda j: filt_z(j, to_z).start())
        table[h, z] = f1c[...]

    def filters_two():
        each(NZ, lambda j: filt_z(j, here).wait_recv())
        filt_h(h).start()

    def filters_three():
        filt_h(1 - h).wait_recv()
        for one in held[5:]:
            one.wait()

    def spectra_one():
        each(NQ, lambda j: spec_f(j, here).wait_recv())
        specall[mine] = specr[0] + specr[1] + specr[2] + specr[3]
        each(PIECES, lambda j: spec_p(j, to_p).start())

    def spectra_two():
        each(PIECES, lambda j: spec_p(j, here).wait_recv())
        low = lax.broadcasted_iota(I32, (SHOTS * COLS, LANES), 1) < BAND

        def both(p, _):
            v = specall[p]
            w = pltpu.roll(v, BAND, 1)
            sa[p] = jnp.where(low, v, w)
            sb[p] = jnp.where(low, -w, v)
            return 0

        lax.fori_loop(0, PIECES, both, 0)

    def ranks():
        rows8[...] = jnp.zeros((SUB, R), I32)
        rows8[0:SHOTS, :] = bins[...].reshape(SHOTS, R)
        rows8[SHOTS : 2 * SHOTS, :] = live[...]
        turned_rows = rows8[...].T
        for s in range(SHOTS):
            bin_col[s] = turned_rows[:, s : s + 1].reshape(PIECES, CHUNKS, SUB, 1)
            live_col[s] = turned_rows[:, SHOTS + s : SHOTS + s + 1].reshape(
                PIECES, CHUNKS, SUB, 1
            )
        for s in range(SHOTS):
            row = bins[s]
            count = jnp.zeros((1, R), I32)
            for o in range(s + 1):
                hit = jnp.where(turned_rows[:, o : o + 1] == row, 1, 0)
                if o == s:
                    before = lax.broadcasted_iota(I32, (R, R), 0) < lax.broadcasted_iota(
                        I32, (R, R), 1
                    )
                    hit = jnp.where(before, hit, 0)
                count = count + jnp.sum(hit, axis=0, keepdims=True)
            slots[:, s * R : (s + 1) * R] = row * 2 + count

    def predict(k):
        each(NZ, lambda j: fourth(k, j, here).wait_recv())
        srot[...] = pltpu.roll(
            ag[k].reshape(NZ * STEPS * PAIR * SUB, LANES), BAND, 1
        ).reshape(NZ, STEPS, PAIR, SUB, LANES)

        def piece(p, _):
            totals = [jnp.zeros((SUB, LANES), F32) for _ in range(SHOTS)]
            for o in range(NZ):
                for b in range(STEPS):
                    for i in range(PAIR):
                        straight, turned = ag[k, o, b, i], srot[o, b, i]
                        for s in range(SHOTS):
                            row = s * COLS + b * POINTS_BLK + o * PAIR + i
                            totals[s] = (
                                totals[s]
                                + sa[p, row : row + 1, :] * straight
                                + sb[p, row : row + 1, :] * turned
                            )
            for s in range(SHOTS):
                pred[p, s, k] = totals[s]
            return 0

        lax.fori_loop(0, PIECES, piece, 0)
        each(PIECES, lambda j: fifth(k, j, to_p).start())
        for s in range(SHOTS):
            bands[f, s, mine, k] = pred[mine, s, k]

    def choose(k):
        own_piece(k).wait()
        each(PIECES, lambda j: first(k, j, here).wait_recv())
        for b in range(STEPS):
            total = jnp.zeros((POINTS_BLK, SUB, LANES), F32)
            for p in range(PIECES):
                total = total + weights[b][p] * r1[k, p]
            m[k, b] = total
        each(NZ, lambda j: second(k, j, to_z).start())
        for b in range(STEPS):
            r2[k, z, b] = m[k, b, pl.ds(z * PAIR, PAIR)]

    def gather(k):
        each(PIECES, lambda j: fifth(k, j, here).wait_recv())
        @pl.when(~inner)
        def _():
            farther(k).start()

        sixth(k, f).start()

    def across(k):
        each(NZ, lambda j: second(k, j, here).wait_recv())
        for b in range(STEPS):
            total = jnp.zeros((PAIR, SUB, LANES), F32)
            for o in range(NZ):
                total = total + weights[b][PIECES + o] * r2[k, o, b]
            hown[k, b] = total
        third(k).start()

    def share(k):
        third(k).wait_recv()
        for b in range(STEPS):
            ag[k, z, b] = (
                weights[b][PIECES + NZ] * hown[k, b] + weights[b][PIECES + NZ + 1] * hin[k, b]
            )
        each(NZ, lambda j: fourth(k, j, to_z).start())

    tile = SHOTS * PIECES * SUB

    def prepare(k):
        lane = lax.broadcasted_iota(I32, (tile, 128), 1)
        one = bin_col[:, :, k].reshape(tile, 1)
        home = one >> 2
        line = ((home >> 1) & 1) * (NZ * PIECES) + ((home >> 2) & (NZ - 1)) * PIECES
        line = line + (home >> 5) * NC + (home & 1)
        pick = jnp.where(lane == line, 1.0, 0.0).astype(B16)
        all_taps = table[...].reshape(128, 128)
        top, rest = split(all_taps)
        middle, last = split(all_taps - top.astype(F32))
        four = dot(pick, top) + (dot(pick, middle) + dot(pick, last))
        start = (one & 3) * TAPS
        four = jnp.where((lane >= start) & (lane < start + TAPS), four, 0.0)
        answer = dot3(four, tap_hi[...], tap_lo[...])
        for o in range(2 * (NQ + 1)):
            factor[k, o] = answer[:, o * LANES : (o + 1) * LANES]

    def filtered(k, order, e_hi, e_lo, c_hi, c_lo):
        ends = jnp.zeros((tile, 128), F32)
        total = jnp.zeros((tile, QUARTER), F32)

        def mix(block, o, span):
            mixed = block * factor[k, o] + pltpu.roll(block, BAND, 1) * factor[k, NQ + 1 + o]
            return dot3(mixed, c_hi[span, :], c_lo[span, :])

        for o in order:
            span = pl.ds(pl.multiple_of(o * LANES, LANES), LANES)
            block = bands[o, :, :, k].reshape(tile, LANES)
            ends = ends + dot3(block, e_hi[span, :], e_lo[span, :])
            total = total + mix(block, o, span)
        return total + mix(ends, NQ, slice(NQ * LANES, (NQ + 1) * LANES))

    def reduce_edge(k):
        @pl.when(inner)
        def _():
            sixth(k, outer).wait_recv()
            sixth(k, NQ - 1 - f).wait_recv()
            sixth(k, NQ - 1 - outer).wait_recv()
            part_out[k] = filtered(
                k, (f, NQ - 1 - f, NQ - 1 - outer),
                out_edge_hi, out_edge_lo, out_combine_hi, out_combine_lo,
            )
            partial_sum(k).start()

    def clean(k):
        def put(total):
            alive = live_col[:, :, k].reshape(tile, 1).astype(F32)
            whole = traces[:, :, k].reshape(tile, QUARTER)
            cleaned[:, :, k] = (alive * (whole - total)).reshape(SHOTS, PIECES, SUB, QUARTER)

        @pl.when(inner)
        def _():
            put(filtered(k, range(NQ), edge_hi, edge_lo, combine_hi, combine_lo))

        @pl.when(~inner)
        def _():
            mine_part = filtered(k, (f,), edge_hi, edge_lo, combine_hi, combine_lo)
            partial_sum(k).wait_recv()
            put(mine_part + part_in[k])

    def stage(t, lag, fn):
        @pl.when((t >= lag) & (t < lag + CHUNKS))
        def _():
            fn(t - lag)

    def tick(t, _):
        stage(t, 0, choose)
        stage(t, 1, share)
        stage(t, 2, predict)
        stage(t, 3, gather)
        stage(t, 4, reduce_edge)
        stage(t, 5, clean)

        @pl.when(t == 0)
        def _():
            filters_one()
            spectra_one()
            ranks()

        @pl.when(t == 1)
        def _():
            filters_two()
            spectra_two()

        @pl.when(t == 2)
        def _():
            filters_three()

        stage(t, 0, across)

        @pl.when(t + AHEAD < CHUNKS)
        def _():
            start_first(t + AHEAD, 0)

        stage(t, 3, prepare)
        return 0

    lax.fori_loop(0, CHUNKS + 5, tick, 0)

    top, rest = split(cleaned[...].reshape(ROWS, QUARTER))
    clean_hi[...] = top
    clean_lo[...] = rest

    me = shot_of(x, z, h, c)
    group = 128 // SUB

    def deal(t):
        return remote(packed.at[t], arrive.at[me], ds, dr.at[me // group], (t, f))

    def place_rows(i, _):
        g = lax.rem(me // group + i, SHARDS // group)
        ids = lax.broadcasted_iota(I32, (128, ROWS), 0) + g * 128
        pick = jnp.where(ids == slots[...], 1.0, 0.0).astype(B16)
        block = dot(pick, clean_hi[...]) + dot(pick, clean_lo[...])
        packed[pl.ds(g * group, group)] = block.reshape(group, SUB, QUARTER)

        def send(j, _):
            t = g * group + lax.rem(me + j, group)

            @pl.when(t != me)
            def _():
                deal(t).start()

            return 0

        lax.fori_loop(0, group, send, 0)
        return 0

    lax.fori_loop(0, SHARDS // group, place_rows, 0)
    arrive[me] = packed[me]

    def finish(k, _):
        each(PIECES, lambda j: first(k, j, to_p).wait_send())
        each(NZ, lambda j: second(k, j, to_z).wait_send())
        third(k).wait_send()
        each(NZ, lambda j: fourth(k, j, to_z).wait_send())
        each(PIECES, lambda j: fifth(k, j, to_p).wait_send())
        sixth(k, f).wait_send()

        @pl.when(~inner)
        def _():
            farther(k).wait_send()

        @pl.when(inner)
        def _():
            partial_sum(k).wait_send()

        return 0

    lax.fori_loop(0, CHUNKS, finish, 0)
    each(NQ, lambda j: spec_f(j, to_f).wait_send())
    each(PIECES, lambda j: spec_p(j, to_p).wait_send())
    each(PIECES, lambda j: filt_p(j, to_p).wait_send())
    each(NZ, lambda j: filt_z(j, to_z).wait_send())
    filt_h(h).wait_send()
    pairs_of = lax.broadcasted_iota(I32, (SUB, QUARTER), 0) // MOST

    def came(g, count):
        some = arrive.at[pl.ds(0, count)]
        pltpu.make_async_copy(some, some, dr.at[g]).wait()

    def sort_group(n, _):
        g = lax.rem(me // group + SHARDS // group - n, SHARDS // group)

        @pl.when(n == 0)
        def _():
            came(g, group - 1)

        @pl.when(n != 0)
        def _():
            came(g, group)

        def sort_rows(s, _):
            i = g * (group // 4) + s
            for b in range(SUB // MOST):
                total = arrive[4 * i]
                if b:
                    total = pltpu.roll(total, SUB - MOST * b, 0)
                for j in range(1, 4):
                    turn = MOST * (j - b) % SUB
                    other = arrive[4 * i + j]
                    if turn:
                        other = pltpu.roll(other, turn, 0)
                    total = jnp.where(pairs_of == j, other, total)
                sorted_rows[b, pl.ds(pl.multiple_of(i * SUB, SUB), SUB), :] = total
            return 0

        lax.fori_loop(0, group // 4, sort_rows, 0)
        return 0

    lax.fori_loop(0, SHARDS // group, sort_group, 0)
    others = packed.at[pl.ds(0, SHARDS - 1)]
    pltpu.make_async_copy(others, others, ds).wait()


def spread(*args):
    dma = pltpu.SemaphoreType.DMA
    v = pltpu.VMEM
    tile = (SUB, LANES)
    vm = pl.BlockSpec(memory_space=pltpu.VMEM)
    sm = pl.BlockSpec(memory_space=pltpu.SMEM)
    hbm = pl.BlockSpec(memory_space=pltpu.HBM)
    small = (STEPS, PAIR, *tile)
    wide = (NQ + 1) * LANES
    return pl.pallas_call(
        spread_kernel,
        out_shape=jax.ShapeDtypeStruct((SUB // MOST, SHARDS * MOST, QUARTER), F32),
        in_specs=[hbm, hbm, hbm, sm, sm] + [hbm] * 9,
        out_specs=vm,
        scratch_shapes=[
            v((SHARDS, SUB, QUARTER), F32), v((SHARDS, SUB, QUARTER), F32),
            v((SHOTS, PIECES, CHUNKS, SUB, QUARTER), F32),
            v((SHOTS, R), I32), v((SHOTS, 1, R), I32), v((4, TAPS), F32),
            v((128, 2 * wide), B16), v((128, 2 * wide), B16),
            v((NQ, SHOTS, PIECES, CHUNKS, *tile), F32),
            v((NH, NZ, PIECES, 128), F32),
            v((QUARTER, NQ * LANES), F32),
            v((NQ * LANES, 128), B16), v((NQ * LANES, 128), B16),
            v((wide, QUARTER), B16), v((wide, QUARTER), B16),
            v((NQ * LANES, 128), B16), v((NQ * LANES, 128), B16),
            v((wide, QUARTER), B16), v((wide, QUARTER), B16),
            v((CHUNKS, SHOTS * PIECES * SUB, QUARTER), F32),
            v((CHUNKS, SHOTS * PIECES * SUB, QUARTER), F32),
            v((COLS, R), F32),
            v((CHUNKS, 2 * (NQ + 1), SHOTS * PIECES * SUB, LANES), F32),
            v((SHOTS, PIECES, CHUNKS, SUB, QUARTER), F32),
            v((ROWS, QUARTER), B16), v((ROWS, QUARTER), B16),
            v((1, ROWS), I32),
            v((SUB, R), I32),
            v((SHOTS, PIECES, CHUNKS, SUB, 1), I32),
            v((SHOTS, PIECES, CHUNKS, SUB, 1), I32),
            v((SUB, 128), F32),
            v((4, PIECES, 128), F32),
            v((CHUNKS, PIECES, POINTS_BLK, *tile), F32),
            v((CHUNKS, STEPS, POINTS_BLK, *tile), F32),
            v((CHUNKS, NZ, *small), F32),
            v((CHUNKS, *small), F32),
            v((CHUNKS, *small), F32),
            v((CHUNKS, NZ, *small), F32),
            v((NQ, SHOTS * COLS, LANES), F32),
            v((NQ, SHOTS * COLS, LANES), F32),
            v((PIECES, SHOTS * COLS, LANES), F32),
            v((PIECES, SHOTS * COLS, LANES), F32),
            v((PIECES, SHOTS * COLS, LANES), F32),
            v((NZ, *small), F32),
            v((PIECES, SHOTS, CHUNKS, *tile), F32),
            v((PIECES, 8, 128), F32),
            v((PIECES, 128), F32),
            dma((CHUNKS, PIECES)), dma((CHUNKS, PIECES)),
            dma((CHUNKS, NZ)), dma((CHUNKS, NZ)),
            dma((CHUNKS,)), dma((CHUNKS,)),
            dma((CHUNKS, NZ)), dma((CHUNKS, NZ)),
            dma((CHUNKS, PIECES)), dma((CHUNKS, PIECES)),
            dma((CHUNKS, 2)), dma((CHUNKS, NQ)),
            dma((CHUNKS,)), dma((CHUNKS,)),
            dma((NQ,)), dma((NQ,)),
            dma((PIECES,)), dma((PIECES,)),
            dma((PIECES,)), dma((PIECES,)),
            dma((NZ,)), dma((NZ,)),
            dma, dma,
            dma((CHUNKS,)),
            dma((15,)),
            dma, dma((8,)),
        ],
        compiler_params=pltpu.CompilerParams(
            collective_id=0, has_side_effects=True, vmem_limit_bytes=60 * 2**20
        ),
    )(*args)


def on_device(traces, live_mask, offset_bin, surface, block_owner, point_column, filters):
    return spread(
        traces.reshape(SHOTS, PIECES, CHUNKS, SUB, QUARTER),
        live_mask,
        offset_bin.reshape(SHOTS, 1, R),
        point_column,
        block_owner,
        surface,
        filters,
        *(jnp.asarray(a) for a in (FORWARD, EDGE_HI, EDGE_LO, COMBINE_HI, COMBINE_LO)),
        jnp.asarray(TAP_HI),
        jnp.asarray(TAP_LO),
    )


def solution(mesh):
    return jax.shard_map(
        on_device,
        mesh=mesh,
        in_specs=(
            P("shot", None, "freq"),
            P("shot", None),
            P("shot", None, None),
            P("shot", None, "freq"),
            P(),
            P(),
            P("shot", None),
        ),
        out_specs=P("shot", None, "freq"),
        check_vma=False,
    )
```
